256 devices in a mesh: side: 2 (over core), grp: 32 (over z, x), tp: 4 (over y).
Axes of the slice: x: 4, y: 4, z: 8, core: 2. Of those that a mesh axis runs over, the one named last changes fastest.
Arguments:
- queries: bfloat16 [128, 32, 128], P('grp', ('side', 'tp')), may hold values from -6 to 6
- new_keys: bfloat16 [128, 32, 128], P('grp', ('side', 'tp')), may hold values from -0.5 to 0.5
- new_values: bfloat16 [128, 32, 128], P('grp', ('side', 'tp')), may hold values from -6 to 6
- kv_memory: float32 [128, 32, 128, 128], P('grp', ('side', 'tp')), may hold values from -0.5 to 0.5
- decay_rate: float32 [32], P(('side', 'tp')), may hold values from 0.3 to 1
- attn_gain: float32 [32, 128], P(('side', 'tp')), may hold values from 0.1 to 1.9
- w_out: bfloat16 [4096, 6144], P(('side', 'tp'), 'grp'), may hold values from -0.09375 to 0.09375
- residual: bfloat16 [128, 6144], P(('side', 'tp'), 'grp'), may hold values from -6 to 6
- moe_gain: float32 [6144], P('grp'), may hold values from 0.1 to 1.9
- w_gate: bfloat16 [32, 6144, 2304], P('grp', None, ('side', 'tp')), may hold values from -0.078125 to 0.078125
- w_up: bfloat16 [32, 6144, 2304], P('grp', None, ('side', 'tp')), may hold values from -0.078125 to 0.078125
- w_down: bfloat16 [32, 2304, 6144], P('grp', ('side', 'tp')), may hold values from -0.09375 to 0.09375
- routes: int32 [128, 2], P(('side', 'tp')), may hold values from 0 to 15, all different within a row; in each aligned block of 16 rows (0 to 15, 16 to 31, ...) at most 4 rows name the same one
- route_weights: float32 [128, 2], P(('side', 'tp')), may hold values from 0.1 to 0.9
Outputs:
- layer_out: bfloat16 [128, 6144], P(('side', 'tp'), 'grp')
The draws below stay inside these ranges and needn't reach their ends.
Inputs may be any that keep to these rules, and one draw needn't show every extreme that they name: `routes`: each row names two different experts; in each aligned block of 16 rows no expert is named by more than 4 rows.
All inputs are finite; a program needn't handle non-finite values.
Results may differ from the reference program's by a relative error of at most 0.0049.
Values may be sent and summed in bfloat16 or wider, within the bound.
No kernel may reach another device: no remote copies, remote signals or barrier semaphores. Data moves between devices by JAX's collectives and lax.ppermute only.
A program may use at most 64 MiB of HBM per device.

```python
import math
import jax
import jax.numpy as jnp
import numpy as np
from jax import lax

D = 6144
HEADS = 32
HEAD_DIM = 128
FF = 4608
SESS = 128
RB = 16
EXPERTS = 16
CAP = 4
N_SIDE = 2
N_TP = 4


def steps_of(own_key, extent, split, low, top_value):
    def one(dim, blocks):
        heights = jax.random.uniform(jax.random.fold_in(jax.random.fold_in(own_key, 6), dim), (blocks,), jnp.float32, low / len(split), top_value / len(split))
        return jnp.repeat(jnp.exp(heights), extent[dim] // blocks).reshape((-1,) + (1,) * (len(extent) - dim - 1))

    gain = one(*split[0])
    for cut in split[1:]:
        gain = gain * one(*cut)
    return gain


def shared_out(rng, own, number, rows, count, top, reach, slope):
    ranking = jax.random.permutation(rng, count)
    crowded, ordinary = load_shares(count, rows * top, reach, slope, True), load_shares(count, rows * top, reach, slope, False)
    places = jnp.arange(count)

    def named(sizes, turn):
        used = int((sizes > 0).sum())
        fixed = max(1, used // 4)
        shifted = fixed + (places - fixed + turn * (used - fixed)) % max(1, count - fixed)
        return jnp.zeros((count,), jnp.int32).at[ranking[jnp.where(places < fixed, places, shifted)]].set(jnp.asarray(sizes, jnp.int32))

    sizes = jnp.where(number % 4 == 0, named(crowded, number // 4), named(ordinary, number - number // 4 - 1))
    mixed = jax.random.permutation(jax.random.fold_in(own, 3), count)
    source_of, taker = mixed[0:count // 2 * 2:2], mixed[1:count // 2 * 2:2]
    room = jnp.minimum(sizes[source_of] - 1, reach - sizes[taker]) // 2
    room = jnp.where((source_of == ranking[0]) | (taker == ranking[0]) | (sizes[taker] == 0), 0, jnp.maximum(room, 0))
    shifted = jax.random.randint(jax.random.fold_in(own, 4), (count // 2,), 0, 1 << 20) % (room + 1)
    sizes = sizes.at[source_of].add(-shifted).at[taker].add(shifted)
    items = jnp.searchsorted(jnp.cumsum(sizes), jnp.arange(rows * top), side="right").astype(jnp.int32)
    grid = items.reshape(top, rows).T
    grid = grid[jax.random.permutation(jax.random.fold_in(own, 1), rows)]
    turn = jax.random.randint(jax.random.fold_in(own, 2), (rows, 1), 0, top)
    return jnp.take_along_axis(grid, (jnp.arange(top)[None, :] + turn) % top, axis=1)


def load_shares(number_of, total, limit, lean, full):
    portions = [(1 << 20) // math.isqrt(standing ** lean) + 1 for standing in range(1, number_of + 1)]
    largest = limit if full else min(limit, max(-(-total // number_of), total * portions[0] // sum(portions)))
    least = 1 if total - largest >= number_of - 1 else 0
    given, rest = [largest] + [least] * (number_of - 1), total - largest - least * (number_of - 1)
    while rest > 0:
        free = [i for i in range(1, number_of) if given[i] < largest] or [i for i in range(1, number_of) if given[i] < limit]
        whole, remaining = sum([portions[i] for i in free]), rest
        for i in free:
            extra = min(limit - given[i], max(1, remaining * portions[i] // whole), rest)
            given[i] = given[i] + extra
            rest = rest - extra
    return np.array(given)


def centred(own_key, dims, deviation, most, cuts=(), kind=jnp.bfloat16):
    array = deviation * jax.random.normal(own_key, dims, jnp.float32)
    if cuts:
        array = array * steps_of(own_key, dims, cuts, -0.22, 0.18)
    return jnp.clip(array, -most, most).astype(kind)


def setup_inputs(seed: int = 0) -> dict:
    streams_of = jax.random.split(jax.random.key(seed), 15)
    queries = centred(streams_of[0], (SESS, HEADS, HEAD_DIM), 1.0, 6.0, ((0, 32), (1, 8)))
    new_keys = centred(streams_of[1], (SESS, HEADS, HEAD_DIM), 0.09, 0.5, ((0, 32), (1, 8)))
    new_values = centred(streams_of[2], (SESS, HEADS, HEAD_DIM), 1.0, 6.0, ((0, 32), (1, 8)))
    kv_memory = centred(streams_of[3], (SESS, HEADS, HEAD_DIM, HEAD_DIM), 0.09, 0.5, ((0, 32), (1, 8)), jnp.float32)
    decay_rate = jnp.clip(0.3 + 0.7 * jax.random.uniform(streams_of[4], (HEADS,), jnp.float32) ** steps_of(streams_of[4], (HEADS,), ((0, 8),), -0.2, 0.2), 0.3, 1.0)
    attn_gain = jnp.clip(1.0 + 0.18 * jax.random.normal(streams_of[5], (HEADS, HEAD_DIM), jnp.float32), 0.1, 1.9)
    w_out = centred(streams_of[6], (HEADS * HEAD_DIM, D), (HEADS * HEAD_DIM) ** -0.5, 0.09375, ((0, 8), (1, 32)))
    residual = centred(streams_of[7], (SESS, D), 1.0, 6.0, ((0, 8), (1, 32)))
    moe_gain = jnp.clip(1.0 + 0.18 * jax.random.normal(streams_of[8], (D,), jnp.float32), 0.1, 1.9)
    w_gate = centred(streams_of[9], (2 * EXPERTS, D, FF // 2), D ** -0.5, 0.078125, ((0, 32), (2, 8)))
    w_up = centred(streams_of[10], (2 * EXPERTS, D, FF // 2), D ** -0.5, 0.078125, ((0, 32), (2, 8)))
    w_down = centred(streams_of[11], (2 * EXPERTS, FF // 2, D), FF ** -0.5, 0.09375, ((0, 32), (1, 8)))
    routes_keys = jax.random.split(jax.random.fold_in(streams_of[12], 1), SESS // RB)
    routes_turns = jax.random.permutation(jax.random.fold_in(streams_of[12], 3), SESS // RB)
    routes = jax.vmap(lambda own, number: shared_out(jax.random.fold_in(streams_of[12], 2), own, number, RB, EXPERTS, 2, CAP, 2))(routes_keys, routes_turns).reshape((SESS, 2))
    route_weights = jnp.clip(0.1 + 0.79999997 * jax.random.uniform(streams_of[13], (SESS, 2), jnp.float32) ** steps_of(streams_of[13], (SESS, 2), ((0, 8),), -0.2, 0.2), 0.1, 0.9)
    return {"queries": queries, "new_keys": new_keys, "new_values": new_values, "kv_memory": kv_memory, "decay_rate": decay_rate, "attn_gain": attn_gain, "w_out": w_out, "residual": residual, "moe_gain": moe_gain, "w_gate": w_gate, "w_up": w_up, "w_down": w_down, "routes": routes, "route_weights": route_weights}


def routing_tables(routes, route_weights, experts, capacity):
    chosen = routes.reshape(-1)
    labels = jnp.arange(experts, dtype=jnp.int32)
    one_hot = (chosen[:, None] == labels[None, :]).astype(jnp.int32)
    running = jnp.cumsum(one_hot, axis=0) - 1
    slot_of = lax.optimization_barrier(jnp.sum(one_hot * running, axis=1))
    position = (chosen * capacity + slot_of).reshape(routes.shape)
    ordered = (slot_of * experts + chosen).reshape(routes.shape)
    places = jnp.arange(experts * capacity, dtype=jnp.int32)
    dispatcher = lax.optimization_barrier(jnp.sum((position[None, :, :] == places[:, None, None]).astype(jnp.float32), axis=2))
    combiner = lax.optimization_barrier(jnp.sum(jnp.where(ordered[:, :, None] == places[None, None, :], route_weights[:, :, None], 0.0), axis=1))
    return (dispatcher, combiner)

def expert_pass(inputs):
    token_rows, gate_pair, up_pair, down_pair = inputs
    summed = jnp.zeros((token_rows.shape[0], D), jnp.float32)
    for which in range(2):
        gate_act = jnp.dot(token_rows, gate_pair[which], preferred_element_type=jnp.float32)
        up_act = jnp.dot(token_rows, up_pair[which], preferred_element_type=jnp.float32)
        hidden = (jax.nn.silu(gate_act) * up_act).astype(jnp.bfloat16)
        summed = summed + jnp.dot(hidden, down_pair[which], preferred_element_type=jnp.float32)
    return summed

def reference(queries, new_keys, new_values, kv_memory, decay_rate, attn_gain, w_out, residual, moe_gain, w_gate, w_up, w_down, routes, route_weights):
    query_f = queries.astype(jnp.float32)
    from_memory = jnp.einsum('shj,shji->shi', query_f, kv_memory, precision=lax.Precision.HIGHEST)
    dot_keys = lax.optimization_barrier(jnp.sum(query_f * new_keys.astype(jnp.float32), axis=2))
    attended = decay_rate[None, :, None] * from_memory + dot_keys[:, :, None] * new_values.astype(jnp.float32)
    mean_sq = lax.optimization_barrier(jnp.mean(attended * attended, axis=(1, 2)))
    head_out = (attended * lax.rsqrt(mean_sq + 1e-06)[:, None, None] * attn_gain[None]).astype(jnp.bfloat16)
    head_out = head_out.reshape(SESS, HEADS * HEAD_DIM)
    hidden_state = residual.astype(jnp.float32) + jnp.dot(head_out, w_out, preferred_element_type=jnp.float32)
    feature_sq = lax.optimization_barrier(jnp.mean(hidden_state * hidden_state, axis=1))
    normed = (hidden_state * lax.rsqrt(feature_sq + 1e-06)[:, None] * moe_gain[None, :]).astype(jnp.bfloat16)
    blocks = N_SIDE * N_TP
    dispatcher, combiner = jax.vmap(lambda r, w: routing_tables(r, w, EXPERTS, CAP))(routes.reshape(blocks, RB, 2), route_weights.reshape(blocks, RB, 2))
    grouped = jnp.einsum('bpr,brd->bpd', dispatcher, normed.reshape(blocks, RB, D).astype(jnp.float32)).astype(jnp.bfloat16)
    grouped = jnp.transpose(grouped.reshape(blocks, EXPERTS, CAP, D), (1, 0, 2, 3)).reshape(EXPERTS, blocks * CAP, D)
    expert_out = lax.map(expert_pass, (grouped, w_gate.reshape(EXPERTS, 2, D, FF // 2), w_up.reshape(EXPERTS, 2, D, FF // 2), w_down.reshape(EXPERTS, 2, FF // 2, D)))
    expert_out = jnp.transpose(expert_out.reshape(EXPERTS, blocks, CAP, D), (1, 2, 0, 3)).reshape(blocks, CAP * EXPERTS, D)
    mixture = jnp.einsum('brp,bpd->brd', combiner, expert_out, precision=lax.Precision.HIGHEST).reshape(SESS, D)
    return (hidden_state + mixture).astype(jnp.bfloat16)
```

```python
import jax
import jax.numpy as jnp
from jax import lax
from jax.sharding import PartitionSpec as P

D = 6144
HEADS = 32
HEAD_DIM = 128
EXPERTS = 16
CAP = 4
RB = 16
LANES = 256

epsilon = 1e-06
BLOCK = ("side", "tp")


def slots(routes):
    one_hot = (routes[..., None] == jnp.arange(EXPERTS, dtype=jnp.int32)).astype(jnp.float32)
    per_row = jnp.sum(one_hot, axis=2)
    rows = jnp.arange(RB)
    earlier = (rows[:, None] > rows[None, :]).astype(jnp.float32)
    counts = jnp.einsum("rq,bqe->bre", earlier, per_row)
    slot = jnp.sum(one_hot * counts[:, :, None, :], axis=3).astype(jnp.int32)
    return one_hot, slot


def halves(value):
    high = lax.reduce_precision(value, 8, 7)
    return high.astype(jnp.bfloat16), (value - high).astype(jnp.bfloat16)


def body(
    queries,
    new_keys,
    new_values,
    kv_memory,
    decay_rate,
    attn_gain,
    w_out,
    residual,
    moe_gain,
    w_gate,
    w_up,
    w_down,
    routes,
    route_weights,
):
    f32, bf16 = jnp.float32, jnp.bfloat16
    groups = lax.axis_size("grp")
    side = lax.axis_index("side")
    tp = lax.axis_index("tp")
    width = residual.shape[1]

    query_f = queries.astype(f32)
    from_memory = jnp.einsum("shj,shji->shi", query_f, kv_memory, precision=lax.Precision.HIGHEST)
    dot_keys = jnp.sum(query_f * new_keys.astype(f32), axis=2)
    attended = decay_rate[None, :, None] * from_memory + dot_keys[:, :, None] * new_values.astype(f32)
    heads = (attended * attn_gain[None]).astype(bf16).reshape(attended.shape[0], -1)

    sent = jnp.broadcast_to(heads[None], (groups,) + heads.shape)
    every = lax.all_to_all(sent, "grp", 0, 0, tiled=True).reshape(-1, heads.shape[1])

    projected = jnp.dot(every, w_out, preferred_element_type=f32)
    plain = every.astype(f32) / attn_gain.reshape(1, -1)
    high, low = halves(jnp.sum(plain * plain, axis=1, keepdims=True))
    spare = LANES - width - 2
    table = jnp.concatenate(
        [projected.astype(bf16), high, low, jnp.zeros((projected.shape[0], spare), bf16)], axis=1
    )
    half = table.shape[0] // 2
    table = jnp.broadcast_to(table.reshape(2, 1, half, LANES), (2, 4, half, LANES)).reshape(8, half, LANES)
    own = jnp.concatenate([residual, routes.astype(bf16), jnp.zeros((RB, spare), bf16)], axis=1)
    message = jnp.concatenate([table, jnp.broadcast_to(own[None], (8, RB, LANES))], axis=1)
    got = lax.all_to_all(message, BLOCK, 0, 0, tiled=True)
    summed = jnp.sum(got[:, :half].astype(f32), axis=0)
    rest = lax.dynamic_slice(got, (4 * side, half, 0), (4, RB, LANES)).reshape(half, LANES)
    inverse_rms = lax.rsqrt((summed[:, width] + summed[:, width + 1]) / (HEADS * HEAD_DIM) + epsilon)
    hidden_state = rest[:, :width].astype(f32) + inverse_rms[:, None] * summed[:, :width]
    feature_high, feature_low = halves(jnp.sum(hidden_state * hidden_state, axis=1, keepdims=True))
    scaled = (hidden_state * moe_gain[None, :]).astype(bf16)
    rows = jnp.concatenate([scaled, feature_high, feature_low, jnp.zeros((half, spare), bf16)], axis=1)

    side_routes = rest[:, width : width + 2].astype(jnp.int32).reshape(4, RB, 2)
    one_hot, slot = slots(side_routes)
    in_slot = (slot[..., None] == jnp.arange(CAP)).astype(f32)
    dispatcher = jnp.einsum("brke,brkc->becr", one_hot, in_slot).astype(bf16)
    grouped = jnp.einsum(
        "becr,brd->ebcd", dispatcher, rows.reshape(4, RB, LANES), preferred_element_type=f32
    ).astype(bf16)
    outbox = jnp.repeat(grouped.reshape(EXPERTS, 4 * CAP, LANES), 2, axis=0)
    inbox = lax.all_to_all(outbox, "grp", 0, 0, tiled=True)
    both = lax.all_gather(inbox, "side", axis=0)
    feature = jnp.sum(both[..., width : width + 2].astype(f32), axis=(1, 3)).reshape(-1, 1)
    scale = lax.rsqrt(feature / D + epsilon)
    tokens = jnp.transpose(both[..., :width], (0, 2, 1, 3)).reshape(-1, D)

    gate_act = scale * jnp.dot(tokens, w_gate[0], preferred_element_type=f32)
    up_act = scale * jnp.dot(tokens, w_up[0], preferred_element_type=f32)
    hidden = (jax.nn.silu(gate_act) * up_act).astype(bf16)
    partial_out = jnp.dot(hidden, w_down[0], preferred_element_type=f32).astype(bf16)
    parts = lax.all_to_all(partial_out.reshape(8, CAP, D), BLOCK, 0, 0, tiled=True)
    expert_sum = jnp.sum(parts.astype(f32), axis=0)
    back = jnp.transpose(expert_sum.reshape(CAP, groups, width), (1, 0, 2))
    returned = lax.all_to_all(back, "grp", 0, 0, tiled=True)

    own_hot, own_slot = slots(routes[None])
    own_in = (own_slot[..., None] == jnp.arange(CAP)).astype(f32)
    combiner = jnp.einsum("brke,brkc,rk->rec", own_hot, own_in, route_weights, precision=lax.Precision.HIGHEST)
    combiner = jnp.repeat(combiner, 2, axis=1).reshape(RB, -1)
    mixture = jnp.dot(combiner, returned.reshape(-1, width), precision=lax.Precision.HIGHEST)
    own_hidden = lax.dynamic_slice(hidden_state, (RB * tp, 0), (RB, width))
    return (own_hidden + mixture).astype(bf16)


def solution(mesh):
    placed = (
        P("grp", ("side", "tp"), None),
        P("grp", ("side", "tp"), None),
        P("grp", ("side", "tp"), None),
        P("grp", ("side", "tp"), None, None),
        P(("side", "tp")),
        P(("side", "tp"), None),
        P(("side", "tp"), "grp"),
        P(("side", "tp"), "grp"),
        P("grp"),
        P("grp", None, ("side", "tp")),
        P("grp", None, ("side", "tp")),
        P("grp", ("side", "tp"), None),
        P(("side", "tp"), None),
        P(("side", "tp"), None),
    )
    return jax.shard_map(
        body, mesh=mesh, in_specs=placed, out_specs=P(("side", "tp"), "grp"), check_vma=False
    )
```

```python
import functools
import jax
import jax.numpy as jnp
from jax import lax
from jax.experimental import pallas as pl
from jax.experimental.pallas import tpu as pltpu
from jax.sharding import PartitionSpec as P

D = 6144
HEADS = 32
HEAD_DIM = 128
EXPERTS = 16
CAP = 4
RB = 16
LANES = 256

epsilon = 1e-06
BLOCK = ("side", "tp")
f32, bf16 = jnp.float32, jnp.bfloat16
VM = pl.BlockSpec(memory_space=pltpu.VMEM)
SM = pl.BlockSpec(memory_space=pltpu.SMEM)
MINOR = (((1,), (1,)), ((), ()))


def iota(shape, dim):
    return lax.broadcasted_iota(jnp.int32, shape, dim)


def column(row, size):
    full = jnp.broadcast_to(row, (size, size))
    return jnp.sum(jnp.where(iota((size, size), 0) == iota((size, size), 1), full, 0.0), axis=1, keepdims=True)


def halves(value):
    high = value.astype(bf16).astype(f32)
    return high, value - high


def attention(q_ref, k_ref, v_ref, kv_ref, decay_ref, gain_ref, out_ref):
    sessions, heads = q_ref.shape[:2]
    query = jnp.concatenate([q_ref[s].astype(f32) for s in range(sessions)], axis=0)
    key = jnp.concatenate([k_ref[s].astype(f32) for s in range(sessions)], axis=0)
    value = jnp.concatenate([v_ref[s].astype(f32) for s in range(sessions)], axis=0)
    turned = jnp.transpose(query)
    dots = jnp.sum(query * key, axis=1, keepdims=True)
    rows = []
    for s in range(sessions):
        for h in range(heads):
            n = s * heads + h
            read = jnp.sum(turned[:, n : n + 1] * kv_ref[s, h], axis=0, keepdims=True)
            rows.append(decay_ref[h] * read)
    attended = jnp.concatenate(rows, axis=0) + dots * value
    gain = jnp.concatenate([gain_ref[...]] * sessions, axis=0)
    message = (attended * gain).astype(bf16)
    for g in range(out_ref.shape[0]):
        out_ref[g] = message


def project(x_ref, w_ref, gain_ref, residual_ref, routes_ref, out_ref, spread_ref):
    heads = gain_ref.shape[0]
    width = w_ref.shape[0]
    total = x_ref.shape[0] * x_ref.shape[1]
    sessions = total // heads
    half = sessions // 2
    spread_ref[...] = x_ref[...].reshape(total, HEAD_DIM).astype(f32)
    lane = iota((1, LANES), 1)
    squares = jnp.zeros((sessions, 1), f32)
    parts = []
    for h in range(heads):
        x = spread_ref[pl.ds(h, sessions, stride=heads), :]
        plain = x / gain_ref[h : h + 1, :]
        squares = squares + jnp.sum(plain * plain, axis=1, keepdims=True)
        parts.append(x.astype(bf16))
    projected = lax.dot_general(jnp.concatenate(parts, axis=1), w_ref[...], MINOR, preferred_element_type=f32)
    high, low = halves(squares)
    pad = jnp.zeros((sessions, LANES - width), f32)
    table = jnp.concatenate([projected, pad], axis=1)
    table = jnp.where(lane == width, high, jnp.where(lane == width + 1, low, table)).astype(bf16)
    routes = routes_ref[...].astype(f32)
    own = jnp.concatenate([residual_ref[...].astype(f32), pad[:RB]], axis=1)
    own = jnp.where(lane == width, column(routes[0:1], RB), jnp.where(lane == width + 1, column(routes[1:2], RB), own))
    own = own.astype(bf16)
    for b in range(8):
        out_ref[b, :half, :] = table[:half] if b < 4 else table[half:]
        out_ref[b, half:, :] = own


def dispatch(x_ref, gain_ref, out_ref, own_ref, scratch_ref):
    width = gain_ref.shape[1]
    half = x_ref.shape[1] - RB
    side, tp, odd = lax.axis_index("side"), lax.axis_index("tp"), lax.rem(lax.axis_index("grp"), 2)
    lane = iota((1, LANES), 1)
    summed = x_ref[0, :half, :].astype(f32)
    for b in range(1, 8):
        summed = summed + x_ref[b, :half, :].astype(f32)
    squares = jnp.sum(jnp.where((lane == width) | (lane == width + 1), summed, 0.0), axis=1, keepdims=True)
    rest = jnp.concatenate([x_ref[4 * side + i, half:, :].astype(f32) for i in range(4)], axis=0)
    hidden = jnp.where(lane < width, rest + lax.rsqrt(squares / (HEADS * HEAD_DIM) + epsilon) * summed, 0.0)
    scratch_ref[...] = hidden
    own_ref[...] = scratch_ref[pl.ds(pl.multiple_of(tp * RB, RB), RB), :]
    high, low = halves(jnp.sum(hidden * hidden, axis=1, keepdims=True))
    gain = jnp.concatenate([gain_ref[...], jnp.zeros((1, LANES - width), f32)], axis=1)
    rows = jnp.where(lane == width, high, jnp.where(lane == width + 1, low, hidden * gain))
    rows = jnp.where(odd == 1, pltpu.roll(rows, LANES - width, 1), rows).astype(bf16)

    first = jnp.sum(jnp.where(lane == width, rest, 0.0), axis=1, keepdims=True).astype(jnp.int32)
    second = jnp.sum(jnp.where(lane == width + 1, rest, 0.0), axis=1, keepdims=True).astype(jnp.int32)
    places = EXPERTS * 4 * CAP
    place = iota((1, places), 1)
    expert = place // (4 * CAP)
    chosen = jnp.where((first == expert) | (second == expert), 1.0, 0.0)
    r, c = iota((half, half), 0), iota((half, half), 1)
    earlier = jnp.where((r // RB == c // RB) & (c < r), 1.0, 0.0).astype(bf16)
    slot = jnp.dot(earlier, chosen.astype(bf16), preferred_element_type=f32)
    block = iota((half, 1), 0) // RB
    here = (slot == (place % CAP).astype(f32)) & (block == place // CAP % 4)
    table = jnp.transpose(jnp.where(here, chosen, 0.0)).astype(bf16)
    routed = jnp.dot(table, rows, preferred_element_type=f32).astype(bf16)
    for e in range(EXPERTS):
        piece = routed[e * 4 * CAP : (e + 1) * 4 * CAP]
        out_ref[2 * e] = piece
        out_ref[2 * e + 1] = piece


def experts(mine_ref, other_ref, gate_ref, up_ref, down_ref, out_ref, x_ref, feature_ref):
    groups, rows, _ = mine_ref.shape
    side = lax.axis_index("side")
    low_lane = iota((rows, 128), 1) < 64
    for ref, at in ((mine_ref, side), (other_ref, 1 - side)):
        start = pl.multiple_of(at * rows, rows)
        feature = jnp.zeros((rows, 128), f32)
        for i in range(groups // 2):
            b_even = ref[2 * i, :, 128:].astype(f32)
            b_odd = ref[2 * i + 1, :, :128].astype(f32)
            feature = feature + jnp.where(low_lane, b_odd, b_even)
            x_ref[pl.ds(start, rows), 384 * i : 384 * i + 128] = ref[2 * i, :, :128]
            x_ref[pl.ds(start, rows), 384 * i + 128 : 384 * i + 256] = jnp.where(low_lane, b_even, b_odd).astype(bf16)
            x_ref[pl.ds(start, rows), 384 * i + 256 : 384 * i + 384] = ref[2 * i + 1, :, 128:]
        feature_ref[pl.ds(start, rows), :] = feature
    scale = lax.rsqrt(jnp.sum(feature_ref[...], axis=1, keepdims=True) / D + epsilon)
    x = x_ref[...]
    gate = scale * lax.dot_general(x, gate_ref[...], MINOR, preferred_element_type=f32)
    up = scale * lax.dot_general(x, up_ref[...], MINOR, preferred_element_type=f32)
    hidden = (gate * jax.nn.sigmoid(gate) * up).astype(bf16)
    span = out_ref.shape[2]
    chunks = [
        jnp.dot(hidden, down_ref[:, q * span : (q + 1) * span], preferred_element_type=f32) for q in range(4)
    ]
    for b in range(8):
        piece = jnp.concatenate([chunk[b * CAP : (b + 1) * CAP] for chunk in chunks], axis=0)
        out_ref[b] = piece.astype(bf16)


def reduce_parts(x_ref, out_ref):
    total = x_ref[0].astype(f32)
    for b in range(1, 8):
        total = total + x_ref[b].astype(f32)
    for q in range(4):
        rows = total[q * CAP : (q + 1) * CAP]
        for i in range(4):
            a, b, c = (rows[:, 384 * i + 128 * n : 384 * i + 128 * (n + 1)] for n in range(3))
            out_ref[q * 8 + 2 * i] = jnp.concatenate([a, b], axis=0)
            out_ref[q * 8 + 2 * i + 1] = jnp.concatenate([b, c], axis=0)


def combiner(routes_ref, weights_ref, a_ref, b_ref):
    routes, weights = routes_ref[...].astype(f32), weights_ref[...]
    r0, r1 = column(routes[0:1], RB).astype(jnp.int32), column(routes[1:2], RB).astype(jnp.int32)
    w0, w1 = column(weights[0:1], RB), column(weights[1:2], RB)
    place = iota((1, 256), 1)
    expert = place // 16
    chosen = jnp.where((r0 == expert) | (r1 == expert), 1.0, 0.0)
    earlier = jnp.where(iota((RB, RB), 1) < iota((RB, RB), 0), 1.0, 0.0)
    slot = jnp.dot(earlier, chosen, preferred_element_type=f32)
    weight = jnp.where(r0 == expert, w0, 0.0) + jnp.where(r1 == expert, w1, 0.0)
    row = (place % 8).astype(f32)
    a_ref[...] = jnp.where(slot == row, weight, 0.0)
    b_ref[...] = jnp.where(slot + CAP == row, weight, 0.0)


def combine(x_ref, a_ref, b_ref, own_ref, out_ref):
    odd = lax.rem(lax.axis_index("grp"), 2)
    width = out_ref.shape[1]
    x = x_ref[...].reshape(-1, 128)
    table = jnp.concatenate([a_ref[...], b_ref[...]], axis=0)
    both = jnp.dot(table, x, precision=lax.Precision.HIGHEST, preferred_element_type=f32)
    mixture = jnp.concatenate([both[:RB], both[RB:]], axis=1)
    mixture = jnp.where(odd == 1, pltpu.roll(mixture, width, 1), mixture)
    out_ref[...] = (own_ref[...] + mixture)[:, :width].astype(bf16)


def call(kernel, outs, specs, args, scratch=(), flops=0, moved=0):
    single = not isinstance(outs, list)
    shapes = [outs] if single else outs
    made = pl.pallas_call(
        kernel,
        out_shape=outs if single else tuple(outs),
        in_specs=specs,
        out_specs=VM if single else tuple(VM for _ in shapes),
        scratch_shapes=list(scratch),
        compiler_params=pltpu.CompilerParams(vmem_limit_bytes=48 * 1024 * 1024),
        cost_estimate=pl.CostEstimate(flops=flops, bytes_accessed=moved, transcendentals=0),
    )
    return made(*args)


def shape(dims, dtype):
    return jax.ShapeDtypeStruct(dims, dtype)


def body(
    queries,
    new_keys,
    new_values,
    kv_memory,
    decay_rate,
    attn_gain,
    w_out,
    residual,
    moe_gain,
    w_gate,
    w_up,
    w_down,
    routes,
    route_weights,
):
    groups = lax.axis_size("grp")
    width = residual.shape[1]
    sessions, heads = queries.shape[:2]
    half = groups * sessions // 2
    turned_routes = routes.T

    comb_a, comb_b = call(
        combiner, [shape((RB, 256), f32)] * 2, [VM, VM], (turned_routes, route_weights.T), flops=10**6, moved=40000
    )
    sent = call(
        attention,
        shape((groups, sessions * heads, HEAD_DIM), bf16),
        [VM, VM, VM, VM, SM, VM],
        (queries, new_keys, new_values, kv_memory, decay_rate, attn_gain),
        flops=10**6,
        moved=1200000,
    )
    every = lax.all_to_all(sent, "grp", 0, 0, tiled=True)
    message = call(
        project,
        shape((8, half + RB, LANES), bf16),
        [VM] * 5,
        (every, w_out.T, attn_gain, residual, turned_routes),
        scratch=[pltpu.VMEM((groups * sessions * heads, HEAD_DIM), f32)],
        flops=25 * 10**6,
        moved=700000,
    )
    got = lax.all_to_all(message, BLOCK, 0, 0, tiled=True)
    outbox, own_hidden = call(
        dispatch,
        [shape((groups, 4 * CAP, LANES), bf16), shape((RB, LANES), f32)],
        [VM, VM],
        (got, moe_gain.reshape(1, -1)),
        scratch=[pltpu.VMEM((half, LANES), f32)],
        flops=10**7,
        moved=700000,
    )
    inbox = lax.all_to_all(outbox, "grp", 0, 0, tiled=True)
    other = lax.ppermute(inbox, "side", [(0, 1), (1, 0)])
    partial_out = call(
        experts,
        shape((8, 4 * CAP, D // 4), bf16),
        [VM] * 5,
        (inbox, other, w_gate[0].T, w_up[0].T, w_down[0]),
        scratch=[pltpu.VMEM((8 * CAP, D), bf16), pltpu.VMEM((8 * CAP, 128), f32)],
        flops=4 * 10**8,
        moved=11000000,
    )
    parts = lax.all_to_all(partial_out, BLOCK, 0, 0, tiled=True)
    back = call(reduce_parts, shape((groups, 2 * CAP, 128), f32), [VM], (parts,), flops=10**6, moved=600000)
    returned = lax.all_to_all(back, "grp", 0, 0, tiled=True)
    return call(
        combine,
        shape((RB, width), bf16),
        [VM] * 4,
        (returned, comb_a, comb_b, own_hidden),
        flops=10**7,
        moved=200000,
    )


def solution(mesh):
    placed = (
        P("grp", ("side", "tp"), None),
        P("grp", ("side", "tp"), None),
        P("grp", ("side", "tp"), None),
        P("grp", ("side", "tp"), None, None),
        P(("side", "tp")),
        P(("side", "tp"), None),
        P(("side", "tp"), "grp"),
        P(("side", "tp"), "grp"),
        P("grp"),
        P("grp", None, ("side", "tp")),
        P("grp", None, ("side", "tp")),
        P("grp", ("side", "tp"), None),
        P(("side", "tp"), None),
        P(("side", "tp"), None),
    )
    return jax.shard_map(
        body, mesh=mesh, in_specs=placed, out_specs=P(("side", "tp"), "grp"), check_vma=False
    )
```

```python
import functools
import jax
import jax.numpy as jnp
from jax import lax
from jax.experimental import pallas as pl
from jax.experimental.pallas import tpu as pltpu
from jax.sharding import PartitionSpec as P

D = 6144
HEADS = 32
HEAD_DIM = 128
EXPERTS = 16
CAP = 4
RB = 16
LANES = 256
DEEP = 6
WIDE = 4

epsilon = 1e-06
BLOCK = ("side", "tp")
f32, bf16 = jnp.float32, jnp.bfloat16
VM = pl.BlockSpec(memory_space=pltpu.VMEM)
HB = pl.BlockSpec(memory_space=pltpu.HBM)
MINOR = (((1,), (1,)), ((), ()))


def iota(shape, dim):
    return lax.broadcasted_iota(jnp.int32, shape, dim)


def column(row, size):
    full = jnp.broadcast_to(row, (size, size))
    return jnp.sum(jnp.where(iota((size, size), 0) == iota((size, size), 1), full, 0.0), axis=1, keepdims=True)


def halves(value):
    high = value.astype(bf16).astype(f32)
    return high, value - high


def attention(
    q_hbm, k_hbm, v_hbm, kv_hbm, decay_hbm, gain_hbm, w_hbm, residual_hbm, moe_hbm, routes_hbm,
    out_ref, w_ref, gain_ref, own_ref, moe_ref,
    q_ref, k_ref, v_ref, kv_ref, decay_ref, residual_ref, routes_ref, narrow_ref, sems,
):
    sessions, heads = q_ref.shape[:2]
    width = residual_ref.shape[1]
    pairs = [(q_hbm, q_ref), (k_hbm, k_ref), (v_hbm, v_ref), (decay_hbm, decay_ref), (gain_hbm, gain_ref)]
    pairs += [(kv_hbm.at[s], kv_ref.at[s]) for s in range(sessions)]
    pairs += [(residual_hbm, residual_ref), (routes_hbm, routes_ref), (moe_hbm, narrow_ref), (w_hbm, w_ref)]
    copies = [pltpu.make_async_copy(source, target, sems.at[i]) for i, (source, target) in enumerate(pairs)]
    for copy in copies:
        copy.start()
    for copy in copies[:5]:
        copy.wait()
    query = jnp.concatenate([q_ref[s].astype(f32) for s in range(sessions)], axis=0)
    key = jnp.concatenate([k_ref[s].astype(f32) for s in range(sessions)], axis=0)
    value = jnp.concatenate([v_ref[s].astype(f32) for s in range(sessions)], axis=0)
    turned = jnp.transpose(query)
    dots = jnp.sum(query * key, axis=1, keepdims=True)
    rows = []
    for s in range(sessions):
        copies[5 + s].wait()
        for h in range(heads):
            n = s * heads + h
            read = jnp.sum(turned[:, n : n + 1] * kv_ref[s, h], axis=0, keepdims=True)
            rows.append(decay_ref[:, h : h + 1] * read)
    attended = jnp.concatenate(rows, axis=0) + dots * value
    gain = jnp.concatenate([gain_ref[...]] * sessions, axis=0)
    message = (attended * gain).astype(bf16)
    for g in range(out_ref.shape[0]):
        out_ref[g] = message

    for copy in copies[5 + sessions :]:
        copy.wait()
    lane = iota((1, LANES), 1)
    routes = routes_ref[...].astype(f32)
    own = jnp.concatenate([residual_ref[...].astype(f32), jnp.zeros((RB, LANES - width), f32)], axis=1)
    own = jnp.where(lane == width, column(routes[0:1], RB), jnp.where(lane == width + 1, column(routes[1:2], RB), own))
    own_ref[...] = own.astype(bf16)
    moe_ref[...] = jnp.concatenate([narrow_ref[...], jnp.zeros((1, LANES - width), f32)], axis=1)


def project(x_ref, w_ref, gain_ref, mine_ref, other_ref, spread_ref):
    heads = gain_ref.shape[0]
    width = w_ref.shape[0]
    total = x_ref.shape[0] * x_ref.shape[1]
    sessions = total // heads
    half = sessions // 2
    spread_ref[...] = x_ref[...].reshape(total, HEAD_DIM).astype(f32)
    lane = iota((1, LANES), 1)
    squares = jnp.zeros((sessions, 1), f32)
    parts = []
    for h in range(heads):
        x = spread_ref[pl.ds(h, sessions, stride=heads), :]
        plain = x / gain_ref[h : h + 1, :]
        squares = squares + jnp.sum(plain * plain, axis=1, keepdims=True)
        parts.append(x.astype(bf16))
    projected = lax.dot_general(jnp.concatenate(parts, axis=1), w_ref[...], MINOR, preferred_element_type=f32)
    table = jnp.concatenate([projected, jnp.zeros((sessions, LANES - width), f32)], axis=1)
    table = jnp.where(lane == width, squares, table)
    first = lax.axis_index("side") == 0
    mine_ref[...] = jnp.where(first, table[:half], table[half:])
    other_ref[...] = jnp.where(first, table[half:], table[:half])


def gather_side(width, mine_ref, other_ref, own_ref, out_ref):
    half = mine_ref.shape[0]
    lane = iota((1, LANES), 1)
    table = mine_ref[...] + other_ref[...]
    squares = jnp.sum(jnp.where(lane == width, table, 0.0), axis=1, keepdims=True)
    high, low = halves(squares)
    table = jnp.where(lane == width, high, jnp.where(lane == width + 1, low, table)).astype(bf16)
    for t in range(out_ref.shape[0]):
        out_ref[t, :half, :] = table
        out_ref[t, half:, :] = own_ref[...]


def dispatch(width, x_ref, gain_ref, out_ref, own_ref, scratch_ref):
    half = x_ref.shape[1] - RB
    tp, odd = lax.axis_index("tp"), lax.rem(lax.axis_index("grp"), 2)
    lane = iota((1, LANES), 1)
    summed = x_ref[0, :half, :].astype(f32)
    for t in range(1, 4):
        summed = summed + x_ref[t, :half, :].astype(f32)
    squares = jnp.sum(jnp.where((lane == width) | (lane == width + 1), summed, 0.0), axis=1, keepdims=True)
    rest = jnp.concatenate([x_ref[t, half:, :].astype(f32) for t in range(4)], axis=0)
    hidden = jnp.where(lane < width, rest + lax.rsqrt(squares / (HEADS * HEAD_DIM) + epsilon) * summed, 0.0)
    scratch_ref[...] = hidden
    own_ref[...] = scratch_ref[pl.ds(pl.multiple_of(tp * RB, RB), RB), :]
    high, low = halves(jnp.sum(hidden * hidden, axis=1, keepdims=True))
    rows = jnp.where(lane == width, high, jnp.where(lane == width + 1, low, hidden * gain_ref[...]))
    rows = jnp.where(odd == 1, pltpu.roll(rows, LANES - width, 1), rows).astype(bf16)

    first = jnp.sum(jnp.where(lane == width, rest, 0.0), axis=1, keepdims=True).astype(jnp.int32)
    second = jnp.sum(jnp.where(lane == width + 1, rest, 0.0), axis=1, keepdims=True).astype(jnp.int32)
    places = EXPERTS * 4 * CAP
    place = iota((1, places), 1)
    expert = place // (4 * CAP)
    chosen = jnp.where((first == expert) | (second == expert), 1.0, 0.0)
    r, c = iota((half, half), 0), iota((half, half), 1)
    earlier = jnp.where((r // RB == c // RB) & (c < r), 1.0, 0.0).astype(bf16)
    slot = jnp.dot(earlier, chosen.astype(bf16), preferred_element_type=f32)
    block = iota((half, 1), 0) // RB
    here = (slot == (place % CAP).astype(f32)) & (block == place // CAP % 4)
    table = jnp.transpose(jnp.where(here, chosen, 0.0)).astype(bf16)
    routed = jnp.dot(table, rows, preferred_element_type=f32).astype(bf16)
    for e in range(EXPERTS):
        piece = routed[e * 4 * CAP : (e + 1) * 4 * CAP]
        out_ref[2 * e] = piece
        out_ref[2 * e + 1] = piece


def experts(
    mine_ref, other_ref, gate_hbm, up_hbm, down_hbm, keep_ref, give_ref,
    x_ref, feature_ref, gate_ref, up_ref, down_ref, sems,
):
    groups, rows, _ = mine_ref.shape
    pairs = []
    for n in range(DEEP):
        part = pl.ds(n * D // DEEP, D // DEEP)
        pairs += [(gate_hbm.at[:, part], gate_ref.at[:, part]), (up_hbm.at[:, part], up_ref.at[:, part])]
    for n in range(WIDE):
        part = pl.ds(n * D // WIDE, D // WIDE)
        pairs.append((down_hbm.at[:, part], down_ref.at[:, part]))
    copies = [pltpu.make_async_copy(source, target, sems.at[i]) for i, (source, target) in enumerate(pairs)]
    for copy in copies:
        copy.start()
    side = lax.axis_index("side")
    low_lane = iota((rows, 128), 1) < 64
    for ref, at in ((mine_ref, side), (other_ref, 1 - side)):
        start = pl.multiple_of(at * rows, rows)
        feature = jnp.zeros((rows, 128), f32)
        for i in range(groups // 2):
            b_even = ref[2 * i, :, 128:].astype(f32)
            b_odd = ref[2 * i + 1, :, :128].astype(f32)
            feature = feature + jnp.where(low_lane, b_odd, b_even)
            x_ref[pl.ds(start, rows), 384 * i : 384 * i + 128] = ref[2 * i, :, :128]
            x_ref[pl.ds(start, rows), 384 * i + 128 : 384 * i + 256] = jnp.where(low_lane, b_even, b_odd).astype(bf16)
            x_ref[pl.ds(start, rows), 384 * i + 256 : 384 * i + 384] = ref[2 * i + 1, :, 128:]
        feature_ref[pl.ds(start, rows), :] = feature
    scale = lax.rsqrt(jnp.sum(feature_ref[...], axis=1, keepdims=True) / D + epsilon)
    gate = jnp.zeros((2 * rows, gate_ref.shape[0]), f32)
    up = gate
    for n in range(DEEP):
        part = slice(n * D // DEEP, (n + 1) * D // DEEP)
        x = x_ref[:, part]
        copies[2 * n].wait()
        gate = gate + lax.dot_general(x, gate_ref[:, part], MINOR, preferred_element_type=f32)
        copies[2 * n + 1].wait()
        up = up + lax.dot_general(x, up_ref[:, part], MINOR, preferred_element_type=f32)
    gate, up = scale * gate, scale * up
    hidden = (gate * jax.nn.sigmoid(gate) * up).astype(bf16)
    first = side == 0
    for n in range(WIDE):
        part = slice(n * D // WIDE, (n + 1) * D // WIDE)
        copies[2 * DEEP + n].wait()
        chunk = jnp.dot(hidden, down_ref[:, part], preferred_element_type=f32)
        keep_ref[:, part] = jnp.where(first, chunk[:rows], chunk[rows:])
        give_ref[:, part] = jnp.where(first, chunk[rows:], chunk[:rows]).astype(bf16)


def spread(keep_ref, other_ref, out_ref):
    for i in range(D // 384):
        a, b, c = (
            keep_ref[:, 128 * n : 128 * n + 128] + other_ref[:, 128 * n : 128 * n + 128].astype(f32)
            for n in range(3 * i, 3 * i + 3)
        )
        for t in range(4):
            rows = slice(t * CAP, (t + 1) * CAP)
            out_ref[(2 * i) * 4 + t] = jnp.concatenate([a[rows], b[rows]], axis=0).astype(bf16)
            out_ref[(2 * i + 1) * 4 + t] = jnp.concatenate([b[rows], c[rows]], axis=0).astype(bf16)


def combiner(routes_ref, weights_ref, out_ref):
    routes, weights = routes_ref[...].astype(f32), weights_ref[...]
    r0, r1 = column(routes[0:1], RB).astype(jnp.int32), column(routes[1:2], RB).astype(jnp.int32)
    w0, w1 = column(weights[0:1], RB), column(weights[1:2], RB)
    place = iota((1, out_ref.shape[1]), 1)
    expert = place // 64
    chosen = jnp.where((r0 == expert) | (r1 == expert), 1.0, 0.0)
    earlier = jnp.where(iota((RB, RB), 1) < iota((RB, RB), 0), 1.0, 0.0)
    slot = jnp.dot(earlier, chosen, preferred_element_type=f32)
    weight = jnp.where(r0 == expert, w0, 0.0) + jnp.where(r1 == expert, w1, 0.0)
    row = (place % 8).astype(f32)
    for part in range(2):
        value = jnp.where(slot + part * CAP == row, weight, 0.0)
        high, rest = halves(value)
        middle, low = halves(rest)
        for n, piece in enumerate((high, middle, low)):
            out_ref[(3 * part + n) * RB : (3 * part + n + 1) * RB, :] = piece.astype(bf16)


def combine(x_ref, table_ref, own_ref, out_ref):
    odd = lax.rem(lax.axis_index("grp"), 2)
    width = out_ref.shape[1]
    x = x_ref[...].reshape(-1, 128)
    both = jnp.dot(table_ref[...], x, preferred_element_type=f32)
    a = both[2 * RB : 3 * RB] + both[RB : 2 * RB] + both[:RB]
    b = both[5 * RB :] + both[4 * RB : 5 * RB] + both[3 * RB : 4 * RB]
    mixture = jnp.concatenate([a, b], axis=1)
    mixture = jnp.where(odd == 1, pltpu.roll(mixture, width, 1), mixture)
    out_ref[...] = (own_ref[...] + mixture)[:, :width].astype(bf16)


def far(x):
    return pltpu.with_memory_space_constraint(x, pltpu.HBM)


def call(kernel, outs, specs, args, scratch=(), flops=0, moved=0, limit=8):
    single = not isinstance(outs, list)
    made = pl.pallas_call(
        kernel,
        out_shape=outs if single else tuple(outs),
        in_specs=specs,
        out_specs=VM if single else tuple(VM for _ in outs),
        scratch_shapes=list(scratch),
        compiler_params=pltpu.CompilerParams(vmem_limit_bytes=limit * 1024 * 1024),
        cost_estimate=pl.CostEstimate(flops=flops, bytes_accessed=moved, transcendentals=0),
    )
    return made(*args)


def shape(dims, dtype):
    return jax.ShapeDtypeStruct(dims, dtype)


def body(
    queries,
    new_keys,
    new_values,
    kv_memory,
    decay_rate,
    attn_gain,
    w_out,
    residual,
    moe_gain,
    w_gate,
    w_up,
    w_down,
    routes,
    route_weights,
):
    groups = lax.axis_size("grp")
    width = residual.shape[1]
    sessions, heads = queries.shape[:2]
    half = groups * sessions // 2
    turned_routes = routes.T
    swap = [(0, 1), (1, 0)]

    table = call(
        combiner, shape((6 * RB, 1024), bf16), [VM, VM], (turned_routes, route_weights.T), flops=10**6, moved=200000
    )
    decay, narrow, w_turned = decay_rate.reshape(1, -1), moe_gain.reshape(1, -1), w_out.T
    taken = (queries, new_keys, new_values, kv_memory, decay, attn_gain, w_turned, residual, narrow, turned_routes)
    held = (queries, new_keys, new_values, kv_memory, decay, residual, turned_routes, narrow)
    taken = tuple(far(x) for x in taken)
    sent, w_near, gain_near, own_rows, moe_near = call(
        attention,
        [
            shape((groups, sessions * heads, HEAD_DIM), bf16),
            shape(w_turned.shape, bf16),
            shape(attn_gain.shape, f32),
            shape((RB, LANES), bf16),
            shape((1, LANES), f32),
        ],
        [HB] * len(taken),
        taken,
        scratch=[pltpu.VMEM(x.shape, x.dtype) for x in held] + [pltpu.SemaphoreType.DMA((9 + sessions,))],
        flops=10**6,
        moved=1200000,
    )
    every = lax.all_to_all(sent, "grp", 0, 0, tiled=True)
    mine, give = call(
        project,
        [shape((half, LANES), f32)] * 2,
        [VM] * 3,
        (every, w_near, gain_near),
        scratch=[pltpu.VMEM((groups * sessions * heads, HEAD_DIM), f32)],
        flops=25 * 10**6,
        moved=700000,
    )
    message = call(
        functools.partial(gather_side, width),
        shape((4, half + RB, LANES), bf16),
        [VM] * 3,
        (mine, lax.ppermute(give, "side", swap), own_rows),
        flops=10**6,
        moved=400000,
    )
    got = lax.all_to_all(message, "tp", 0, 0, tiled=True)
    outbox, own_hidden = call(
        functools.partial(dispatch, width),
        [shape((groups, 4 * CAP, LANES), bf16), shape((RB, LANES), f32)],
        [VM, VM],
        (got, moe_near),
        scratch=[pltpu.VMEM((half, LANES), f32)],
        flops=10**7,
        moved=700000,
    )
    inbox = lax.all_to_all(outbox, "grp", 0, 0, tiled=True)
    weights = [far(x) for x in (w_gate[0].T, w_up[0].T, w_down[0])]
    keep, give = call(
        experts,
        [shape((4 * CAP, D), f32), shape((4 * CAP, D), bf16)],
        [VM, VM, HB, HB, HB],
        (inbox, lax.ppermute(inbox, "side", swap), *weights),
        scratch=[pltpu.VMEM((8 * CAP, D), bf16), pltpu.VMEM((8 * CAP, 128), f32)]
        + [pltpu.VMEM(x.shape, bf16) for x in weights]
        + [pltpu.SemaphoreType.DMA((2 * DEEP + WIDE,))],
        flops=4 * 10**8,
        moved=11000000,
        limit=24,
    )
    back = call(
        spread,
        shape((groups * 4, 2 * CAP, 128), bf16),
        [VM, VM],
        (keep, lax.ppermute(give, "side", swap)),
        flops=10**6,
        moved=900000,
    )
    returned = lax.all_to_all(back, ("grp", "tp"), 0, 0, tiled=True)
    return call(
        combine,
        shape((RB, width), bf16),
        [VM] * 3,
        (returned, table, own_hidden),
        flops=3 * 10**7,
        moved=500000,
    )


def solution(mesh):
    placed = (
        P("grp", ("side", "tp"), None),
        P("grp", ("side", "tp"), None),
        P("grp", ("side", "tp"), None),
        P("grp", ("side", "tp"), None, None),
        P(("side", "tp")),
        P(("side", "tp"), None),
        P(("side", "tp"), "grp"),
        P(("side", "tp"), "grp"),
        P("grp"),
        P("grp", None, ("side", "tp")),
        P("grp", None, ("side", "tp")),
        P("grp", ("side", "tp"), None),
        P(("side", "tp"), None),
        P(("side", "tp"), None),
    )
    return jax.shard_map(
        body, mesh=mesh, in_specs=placed, out_specs=P(("side", "tp"), "grp"), check_vma=False
    )
```

```python
import functools
import jax
import jax.numpy as jnp
from jax import lax
from jax.experimental import pallas as pl
from jax.experimental.pallas import tpu as pltpu
from jax.sharding import PartitionSpec as P

D = 6144
HEADS = 32
HEAD_DIM = 128
EXPERTS = 16
CAP = 4
RB = 16
LANES = 256
DEEP = 6
WIDE = 4

epsilon = 1e-06
BLOCK = ("side", "tp")
f32, bf16 = jnp.float32, jnp.bfloat16
VM = pl.BlockSpec(memory_space=pltpu.VMEM)
HB = pl.BlockSpec(memory_space=pltpu.HBM)
MINOR = (((1,), (1,)), ((), ()))


def iota(shape, dim):
    return lax.broadcasted_iota(jnp.int32, shape, dim)


def column(row, size):
    full = jnp.broadcast_to(row, (size, size))
    return jnp.sum(jnp.where(iota((size, size), 0) == iota((size, size), 1), full, 0.0), axis=1, keepdims=True)


def halves(value):
    high = value.astype(bf16).astype(f32)
    return high, value - high


def attention(
    q_hbm, k_hbm, v_hbm, kv_hbm, decay_hbm, gain_hbm, w_hbm, residual_hbm, moe_hbm, routes_hbm, weights_hbm,
    out_ref, w_ref, gain_ref, own_ref, moe_ref, table_ref,
    q_ref, k_ref, v_ref, kv_ref, decay_ref, residual_ref, routes_ref, weights_ref, narrow_ref, sems,
):
    sessions, heads = q_ref.shape[:2]
    width = residual_ref.shape[1]
    pairs = [(routes_hbm, routes_ref), (weights_hbm, weights_ref), (residual_hbm, residual_ref)]
    pairs += [(q_hbm, q_ref), (k_hbm, k_ref), (v_hbm, v_ref), (decay_hbm, decay_ref), (gain_hbm, gain_ref)]
    pairs += [(kv_hbm.at[s], kv_ref.at[s]) for s in range(sessions)]
    pairs += [(moe_hbm, narrow_ref), (w_hbm, w_ref)]
    copies = [pltpu.make_async_copy(source, target, sems.at[i]) for i, (source, target) in enumerate(pairs)]
    for copy in copies:
        copy.start()
    for copy in copies[:3]:
        copy.wait()
    routes = routes_ref[...].astype(f32)
    combiner(routes, weights_ref[...], table_ref)
    lane = iota((1, LANES), 1)
    own = jnp.concatenate([residual_ref[...].astype(f32), jnp.zeros((RB, LANES - width), f32)], axis=1)
    own = jnp.where(lane == width, column(routes[0:1], RB), jnp.where(lane == width + 1, column(routes[1:2], RB), own))
    own_ref[...] = own.astype(bf16)
    for copy in copies[3:8]:
        copy.wait()
    query = jnp.concatenate([q_ref[s].astype(f32) for s in range(sessions)], axis=0)
    key = jnp.concatenate([k_ref[s].astype(f32) for s in range(sessions)], axis=0)
    value = jnp.concatenate([v_ref[s].astype(f32) for s in range(sessions)], axis=0)
    turned = jnp.transpose(query)
    dots = jnp.sum(query * key, axis=1, keepdims=True)
    rows = []
    for s in range(sessions):
        copies[8 + s].wait()
        for h in range(heads):
            n = s * heads + h
            read = jnp.sum(turned[:, n : n + 1] * kv_ref[s, h], axis=0, keepdims=True)
            rows.append(decay_ref[:, h : h + 1] * read)
    attended = jnp.concatenate(rows, axis=0) + dots * value
    gain = jnp.concatenate([gain_ref[...]] * sessions, axis=0)
    message = (attended * gain).astype(bf16)
    for g in range(out_ref.shape[0]):
        out_ref[g] = message

    for copy in copies[8 + sessions :]:
        copy.wait()
    moe_ref[...] = jnp.concatenate([narrow_ref[...], jnp.zeros((1, LANES - width), f32)], axis=1)


def project(x_ref, w_ref, gain_ref, mine_ref, other_ref, spread_ref):
    heads = gain_ref.shape[0]
    width = w_ref.shape[0]
    total = x_ref.shape[0] * x_ref.shape[1]
    sessions = total // heads
    half = sessions // 2
    spread_ref[...] = x_ref[...].reshape(total, HEAD_DIM).astype(f32)
    lane = iota((1, LANES), 1)
    squares = jnp.zeros((sessions, 1), f32)
    parts = []
    for h in range(heads):
        x = spread_ref[pl.ds(h, sessions, stride=heads), :]
        plain = x / gain_ref[h : h + 1, :]
        squares = squares + jnp.sum(plain * plain, axis=1, keepdims=True)
        parts.append(x.astype(bf16))
    projected = lax.dot_general(jnp.concatenate(parts, axis=1), w_ref[...], MINOR, preferred_element_type=f32)
    table = jnp.concatenate([projected, jnp.zeros((sessions, LANES - width), f32)], axis=1)
    table = jnp.where(lane == width, squares, table)
    first = lax.axis_index("side") == 0
    mine_ref[...] = jnp.where(first, table[:half], table[half:])
    other_ref[...] = jnp.where(first, table[half:], table[:half])


def gather_side(width, mine_ref, other_ref, own_ref, out_ref):
    half = mine_ref.shape[0]
    lane = iota((1, LANES), 1)
    table = mine_ref[...] + other_ref[...]
    squares = jnp.sum(jnp.where(lane == width, table, 0.0), axis=1, keepdims=True)
    high, low = halves(squares)
    table = jnp.where(lane == width, high, jnp.where(lane == width + 1, low, table)).astype(bf16)
    for t in range(out_ref.shape[0]):
        out_ref[t, :half, :] = table
        out_ref[t, half:, :] = own_ref[...]


def dispatch(width, x_ref, gain_ref, out_ref, own_ref, scratch_ref):
    half = x_ref.shape[1] - RB
    tp, odd = lax.axis_index("tp"), lax.rem(lax.axis_index("grp"), 2)
    lane = iota((1, LANES), 1)
    summed = x_ref[0, :half, :].astype(f32)
    for t in range(1, 4):
        summed = summed + x_ref[t, :half, :].astype(f32)
    squares = jnp.sum(jnp.where((lane == width) | (lane == width + 1), summed, 0.0), axis=1, keepdims=True)
    rest = jnp.concatenate([x_ref[t, half:, :].astype(f32) for t in range(4)], axis=0)
    hidden = jnp.where(lane < width, rest + lax.rsqrt(squares / (HEADS * HEAD_DIM) + epsilon) * summed, 0.0)
    scratch_ref[...] = hidden
    own_ref[...] = scratch_ref[pl.ds(pl.multiple_of(tp * RB, RB), RB), :]
    high, low = halves(jnp.sum(hidden * hidden, axis=1, keepdims=True))
    rows = jnp.where(lane == width, high, jnp.where(lane == width + 1, low, hidden * gain_ref[...]))
    rows = jnp.where(odd == 1, pltpu.roll(rows, LANES - width, 1), rows).astype(bf16)

    first = jnp.sum(jnp.where(lane == width, rest, 0.0), axis=1, keepdims=True).astype(jnp.int32)
    second = jnp.sum(jnp.where(lane == width + 1, rest, 0.0), axis=1, keepdims=True).astype(jnp.int32)
    places = EXPERTS * 4 * CAP
    place = iota((1, places), 1)
    expert = place // (4 * CAP)
    chosen = jnp.where((first == expert) | (second == expert), 1.0, 0.0)
    r, c = iota((half, half), 0), iota((half, half), 1)
    earlier = jnp.where((r // RB == c // RB) & (c < r), 1.0, 0.0).astype(bf16)
    slot = jnp.dot(earlier, chosen.astype(bf16), preferred_element_type=f32)
    block = iota((half, 1), 0) // RB
    here = (slot == (place % CAP).astype(f32)) & (block == place // CAP % 4)
    table = jnp.transpose(jnp.where(here, chosen, 0.0)).astype(bf16)
    routed = jnp.dot(table, rows, preferred_element_type=f32).astype(bf16)
    for e in range(EXPERTS):
        piece = routed[e * 4 * CAP : (e + 1) * 4 * CAP]
        out_ref[2 * e] = piece
        out_ref[2 * e + 1] = piece


def prefetch(after_ref, far_ref, near_ref, token_ref, sem):
    copy = pltpu.make_async_copy(far_ref, near_ref, sem)
    copy.start()
    token_ref[...] = jnp.zeros_like(token_ref)
    copy.wait()


def experts(mine_ref, other_ref, gate_ref, up_ref, down_ref, keep_ref, give_ref, x_ref, feature_ref):
    groups, rows, _ = mine_ref.shape
    side = lax.axis_index("side")
    low_lane = iota((rows, 128), 1) < 64
    for ref, at in ((mine_ref, side), (other_ref, 1 - side)):
        start = pl.multiple_of(at * rows, rows)
        feature = jnp.zeros((rows, 128), f32)
        for i in range(groups // 2):
            b_even = ref[2 * i, :, 128:].astype(f32)
            b_odd = ref[2 * i + 1, :, :128].astype(f32)
            feature = feature + jnp.where(low_lane, b_odd, b_even)
            x_ref[pl.ds(start, rows), 384 * i : 384 * i + 128] = ref[2 * i, :, :128]
            x_ref[pl.ds(start, rows), 384 * i + 128 : 384 * i + 256] = jnp.where(low_lane, b_even, b_odd).astype(bf16)
            x_ref[pl.ds(start, rows), 384 * i + 256 : 384 * i + 384] = ref[2 * i + 1, :, 128:]
        feature_ref[pl.ds(start, rows), :] = feature
    scale = lax.rsqrt(jnp.sum(feature_ref[...], axis=1, keepdims=True) / D + epsilon)
    gate = jnp.zeros((2 * rows, gate_ref.shape[0]), f32)
    up = gate
    for n in range(DEEP):
        part = slice(n * D // DEEP, (n + 1) * D // DEEP)
        x = x_ref[:, part]
        gate = gate + lax.dot_general(x, gate_ref[:, part], MINOR, preferred_element_type=f32)
        up = up + lax.dot_general(x, up_ref[:, part], MINOR, preferred_element_type=f32)
    gate, up = scale * gate, scale * up
    hidden = (gate * jax.nn.sigmoid(gate) * up).astype(bf16)
    first = side == 0
    for n in range(WIDE):
        part = slice(n * D // WIDE, (n + 1) * D // WIDE)
        chunk = jnp.dot(hidden, down_ref[:, part], preferred_element_type=f32)
        keep_ref[:, part] = jnp.where(first, chunk[:rows], chunk[rows:])
        give_ref[:, part] = jnp.where(first, chunk[rows:], chunk[:rows]).astype(bf16)


def spread(keep_ref, other_ref, out_ref):
    for i in range(D // 384):
        a, b, c = (
            keep_ref[:, 128 * n : 128 * n + 128] + other_ref[:, 128 * n : 128 * n + 128].astype(f32)
            for n in range(3 * i, 3 * i + 3)
        )
        for t in range(4):
            rows = slice(t * CAP, (t + 1) * CAP)
            out_ref[(2 * i) * 4 + t] = jnp.concatenate([a[rows], b[rows]], axis=0).astype(bf16)
            out_ref[(2 * i + 1) * 4 + t] = jnp.concatenate([b[rows], c[rows]], axis=0).astype(bf16)


def combiner(routes, weights, out_ref):
    r0, r1 = column(routes[0:1], RB).astype(jnp.int32), column(routes[1:2], RB).astype(jnp.int32)
    w0, w1 = column(weights[0:1], RB), column(weights[1:2], RB)
    place = iota((1, out_ref.shape[1]), 1)
    expert = place // 64
    chosen = jnp.where((r0 == expert) | (r1 == expert), 1.0, 0.0)
    earlier = jnp.where(iota((RB, RB), 1) < iota((RB, RB), 0), 1.0, 0.0)
    slot = jnp.dot(earlier, chosen, preferred_element_type=f32)
    weight = jnp.where(r0 == expert, w0, 0.0) + jnp.where(r1 == expert, w1, 0.0)
    row = (place % 8).astype(f32)
    for part in range(2):
        value = jnp.where(slot + part * CAP == row, weight, 0.0)
        high, rest = halves(value)
        middle, low = halves(rest)
        for n, piece in enumerate((high, middle, low)):
            out_ref[(3 * part + n) * RB : (3 * part + n + 1) * RB, :] = piece.astype(bf16)


def combine(x_ref, table_ref, own_ref, out_ref):
    odd = lax.rem(lax.axis_index("grp"), 2)
    width = out_ref.shape[1]
    x = x_ref[...].reshape(-1, 128)
    both = jnp.dot(table_ref[...], x, preferred_element_type=f32)
    a = both[2 * RB : 3 * RB] + both[RB : 2 * RB] + both[:RB]
    b = both[5 * RB :] + both[4 * RB : 5 * RB] + both[3 * RB : 4 * RB]
    mixture = jnp.concatenate([a, b], axis=1)
    mixture = jnp.where(odd == 1, pltpu.roll(mixture, width, 1), mixture)
    out_ref[...] = (own_ref[...] + mixture)[:, :width].astype(bf16)


def far(x):
    return pltpu.with_memory_space_constraint(x, pltpu.HBM)


def call(kernel, outs, specs, args, scratch=(), flops=0, moved=0, limit=8):
    single = not isinstance(outs, list)
    made = pl.pallas_call(
        kernel,
        out_shape=outs if single else tuple(outs),
        in_specs=specs,
        out_specs=VM if single else tuple(VM for _ in outs),
        scratch_shapes=list(scratch),
        compiler_params=pltpu.CompilerParams(vmem_limit_bytes=limit * 1024 * 1024),
        cost_estimate=pl.CostEstimate(flops=flops, bytes_accessed=moved, transcendentals=0),
    )
    return made(*args)


def fetch(after, x):
    near, token = call(
        prefetch,
        [pltpu.VMEM(x.shape, x.dtype), shape((8, 128), f32)],
        [VM, HB],
        (after, far(x)),
        scratch=[pltpu.SemaphoreType.DMA],
        moved=4 * x.size,
    )
    return pltpu.with_memory_space_constraint(near, pltpu.VMEM), token


def shape(dims, dtype):
    return jax.ShapeDtypeStruct(dims, dtype)


def body(
    queries,
    new_keys,
    new_values,
    kv_memory,
    decay_rate,
    attn_gain,
    w_out,
    residual,
    moe_gain,
    w_gate,
    w_up,
    w_down,
    routes,
    route_weights,
):
    groups = lax.axis_size("grp")
    width = residual.shape[1]
    sessions, heads = queries.shape[:2]
    half = groups * sessions // 2
    turned_routes = routes.T
    swap = [(0, 1), (1, 0)]

    decay, narrow, w_turned = decay_rate.reshape(1, -1), moe_gain.reshape(1, -1), w_out.T
    taken = (queries, new_keys, new_values, kv_memory, decay, attn_gain, w_turned, residual, narrow, turned_routes, route_weights.T)
    held = (queries, new_keys, new_values, kv_memory, decay, residual, turned_routes, route_weights.T, narrow)
    taken = tuple(far(x) for x in taken)
    sent, w_near, gain_near, own_rows, moe_near, table = call(
        attention,
        [
            shape((groups, sessions * heads, HEAD_DIM), bf16),
            shape(w_turned.shape, bf16),
            shape(attn_gain.shape, f32),
            shape((RB, LANES), bf16),
            shape((1, LANES), f32),
            shape((6 * RB, 1024), bf16),
        ],
        [HB] * len(taken),
        taken,
        scratch=[pltpu.VMEM(x.shape, x.dtype) for x in held] + [pltpu.SemaphoreType.DMA((10 + sessions,))],
        flops=10**6,
        moved=1200000,
    )
    every = lax.all_to_all(sent, "grp", 0, 0, tiled=True)
    mine, give = call(
        project,
        [shape((half, LANES), f32)] * 2,
        [VM] * 3,
        (every, w_near, gain_near),
        scratch=[pltpu.VMEM((groups * sessions * heads, HEAD_DIM), f32)],
        flops=25 * 10**6,
        moved=700000,
    )
    message = call(
        functools.partial(gather_side, width),
        shape((4, half + RB, LANES), bf16),
        [VM] * 3,
        (mine, lax.ppermute(give, "side", swap), own_rows),
        flops=10**6,
        moved=400000,
    )
    got = lax.all_to_all(message, "tp", 0, 0, tiled=True)
    outbox, own_hidden = call(
        functools.partial(dispatch, width),
        [shape((groups, 4 * CAP, LANES), bf16), shape((RB, LANES), f32)],
        [VM, VM],
        (got, moe_near),
        scratch=[pltpu.VMEM((half, LANES), f32)],
        flops=3 * 10**10,
        moved=700000,
    )
    inbox = lax.all_to_all(outbox, "grp", 0, 0, tiled=True)
    keep, give = call(
        experts,
        [shape((4 * CAP, D), f32), shape((4 * CAP, D), bf16)],
        [VM] * 5,
        (inbox, lax.ppermute(inbox, "side", swap), w_gate[0].T, w_up[0].T, w_down[0]),
        scratch=[pltpu.VMEM((8 * CAP, D), bf16), pltpu.VMEM((8 * CAP, 128), f32)],
        flops=4 * 10**8,
        moved=11000000,
        limit=12,
    )
    back = call(
        spread,
        shape((groups * 4, 2 * CAP, 128), bf16),
        [VM, VM],
        (keep, lax.ppermute(give, "side", swap)),
        flops=10**6,
        moved=900000,
    )
    returned = lax.all_to_all(back, ("grp", "tp"), 0, 0, tiled=True)
    return call(
        combine,
        shape((RB, width), bf16),
        [VM] * 3,
        (returned, table, own_hidden),
        flops=3 * 10**7,
        moved=500000,
    )


def solution(mesh):
    placed = (
        P("grp", ("side", "tp"), None),
        P("grp", ("side", "tp"), None),
        P("grp", ("side", "tp"), None),
        P("grp", ("side", "tp"), None, None),
        P(("side", "tp")),
        P(("side", "tp"), None),
        P(("side", "tp"), "grp"),
        P(("side", "tp"), "grp"),
        P("grp"),
        P("grp", None, ("side", "tp")),
        P("grp", None, ("side", "tp")),
        P("grp", ("side", "tp"), None),
        P(("side", "tp"), None),
        P(("side", "tp"), None),
    )
    return jax.shard_map(
        body, mesh=mesh, in_specs=placed, out_specs=P(("side", "tp"), "grp"), check_vma=False
    )
```

```python
import functools
import jax
import jax.numpy as jnp
from jax import lax
from jax.experimental import pallas as pl
from jax.experimental.pallas import tpu as pltpu
from jax.sharding import PartitionSpec as P

D = 6144
HEADS = 32
HEAD_DIM = 128
EXPERTS = 16
CAP = 4
RB = 16
LANES = 256
DEEP = 6
WIDE = 8

STEPS = (1, 3, 2)

epsilon = 1e-06
f32, bf16 = jnp.float32, jnp.bfloat16
VM = pl.BlockSpec(memory_space=pltpu.VMEM)
HB = pl.BlockSpec(memory_space=pltpu.HBM)
MINOR = (((1,), (1,)), ((), ()))


def iota(shape, dim):
    return lax.broadcasted_iota(jnp.int32, shape, dim)


def column(row, size):
    full = jnp.broadcast_to(row, (size, size))
    return jnp.sum(jnp.where(iota((size, size), 0) == iota((size, size), 1), full, 0.0), axis=1, keepdims=True)


def halves(value):
    high = value.astype(bf16).astype(f32)
    return high, value - high


def attention(
    q_hbm, k_hbm, v_hbm, kv_hbm, decay_hbm, gain_hbm, w_hbm, residual_hbm, moe_hbm, routes_hbm, weights_hbm,
    out_ref, w_ref, gain_ref, own_ref, moe_ref, table_ref,
    q_ref, k_ref, v_ref, kv_ref, decay_ref, residual_ref, routes_ref, weights_ref, narrow_ref, sems,
):
    sessions, heads = q_ref.shape[:2]
    width = residual_ref.shape[1]
    pairs = [(routes_hbm, routes_ref), (weights_hbm, weights_ref), (residual_hbm, residual_ref)]
    pairs += [(q_hbm, q_ref), (k_hbm, k_ref), (v_hbm, v_ref), (decay_hbm, decay_ref), (gain_hbm, gain_ref)]
    pairs += [(kv_hbm.at[s], kv_ref.at[s]) for s in range(sessions)]
    pairs += [(moe_hbm, narrow_ref), (w_hbm, w_ref)]
    copies = [pltpu.make_async_copy(source, target, sems.at[i]) for i, (source, target) in enumerate(pairs)]
    for copy in copies:
        copy.start()
    for copy in copies[:3]:
        copy.wait()
    routes = routes_ref[...].astype(f32)
    combiner(routes, weights_ref[...], table_ref)
    lane = iota((1, LANES), 1)
    own = jnp.concatenate([residual_ref[...].astype(f32), jnp.zeros((RB, LANES - width), f32)], axis=1)
    own = jnp.where(lane == width, column(routes[0:1], RB), jnp.where(lane == width + 1, column(routes[1:2], RB), own))
    own_ref[...] = own.astype(bf16)
    for copy in copies[3:8]:
        copy.wait()
    query = jnp.concatenate([q_ref[s].astype(f32) for s in range(sessions)], axis=0)
    key = jnp.concatenate([k_ref[s].astype(f32) for s in range(sessions)], axis=0)
    value = jnp.concatenate([v_ref[s].astype(f32) for s in range(sessions)], axis=0)
    turned = jnp.transpose(query)
    dots = jnp.sum(query * key, axis=1, keepdims=True)
    rows = []
    for s in range(sessions):
        copies[8 + s].wait()
        for h in range(heads):
            n = s * heads + h
            read = jnp.sum(turned[:, n : n + 1] * kv_ref[s, h], axis=0, keepdims=True)
            rows.append(decay_ref[:, h : h + 1] * read)
    attended = jnp.concatenate(rows, axis=0) + dots * value
    gain = jnp.concatenate([gain_ref[...]] * sessions, axis=0)
    message = (attended * gain).astype(bf16)
    for g in range(out_ref.shape[0]):
        out_ref[g] = message

    for copy in copies[8 + sessions :]:
        copy.wait()
    moe_ref[...] = jnp.concatenate([narrow_ref[...], jnp.zeros((1, LANES - width), f32)], axis=1)


def project(x_ref, w_ref, gain_ref, mine_ref, other_ref, spread_ref):
    heads = gain_ref.shape[0]
    width = w_ref.shape[0]
    total = x_ref.shape[0] * x_ref.shape[1]
    sessions = total // heads
    half = sessions // 2
    spread_ref[...] = x_ref[...].reshape(total, HEAD_DIM).astype(f32)
    lane = iota((1, LANES), 1)
    squares = jnp.zeros((sessions, 1), f32)
    parts = []
    for h in range(heads):
        x = spread_ref[pl.ds(h, sessions, stride=heads), :]
        plain = x / gain_ref[h : h + 1, :]
        squares = squares + jnp.sum(plain * plain, axis=1, keepdims=True)
        parts.append(x.astype(bf16))
    projected = lax.dot_general(jnp.concatenate(parts, axis=1), w_ref[...], MINOR, preferred_element_type=f32)
    table = jnp.concatenate([projected, jnp.zeros((sessions, LANES - width), f32)], axis=1)
    table = jnp.where(lane == width, squares, table)
    first = lax.axis_index("side") == 0
    mine_ref[...] = jnp.where(first, table[:half], table[half:])
    other_ref[...] = jnp.where(first, table[half:], table[:half])


def gather_side(width, mine_ref, other_ref, own_ref, out_ref, sum_ref):
    half = mine_ref.shape[0]
    lane = iota((1, LANES), 1)
    table = mine_ref[...] + other_ref[...]
    sum_ref[...] = table
    squares = jnp.sum(jnp.where(lane == width, table, 0.0), axis=1, keepdims=True)
    high, low = halves(squares)
    table = jnp.where(lane == width, high, jnp.where(lane == width + 1, low, table)).astype(bf16)
    out_ref[:half, :] = table
    out_ref[half:, :] = own_ref[...]


def dispatch(width, sum_ref, mine_ref, a_ref, b_ref, c_ref, gain_ref, out_ref, own_ref, rest_ref, scratch_ref):
    half = sum_ref.shape[0]
    tp, odd = lax.axis_index("tp"), lax.rem(lax.axis_index("grp"), 2)
    lane = iota((1, LANES), 1)
    summed = sum_ref[...]
    rest_ref[pl.ds(pl.multiple_of(tp * RB, RB), RB), :] = mine_ref[...].astype(f32)
    for step, ref in zip(STEPS, (a_ref, b_ref, c_ref)):
        summed = summed + ref[:half, :].astype(f32)
        source = lax.rem(tp + 4 - step, 4)
        rest_ref[pl.ds(pl.multiple_of(source * RB, RB), RB), :] = ref[half:, :].astype(f32)
    squares = jnp.sum(jnp.where((lane == width) | (lane == width + 1), summed, 0.0), axis=1, keepdims=True)
    rest = rest_ref[...]
    hidden = jnp.where(lane < width, rest + lax.rsqrt(squares / (HEADS * HEAD_DIM) + epsilon) * summed, 0.0)
    scratch_ref[...] = hidden
    own_ref[...] = scratch_ref[pl.ds(pl.multiple_of(tp * RB, RB), RB), :]
    high, low = halves(jnp.sum(hidden * hidden, axis=1, keepdims=True))
    rows = jnp.where(lane == width, high, jnp.where(lane == width + 1, low, hidden * gain_ref[...]))
    rows = jnp.where(odd == 1, pltpu.roll(rows, LANES - width, 1), rows).astype(bf16)

    first = jnp.sum(jnp.where(lane == width, rest, 0.0), axis=1, keepdims=True).astype(jnp.int32)
    second = jnp.sum(jnp.where(lane == width + 1, rest, 0.0), axis=1, keepdims=True).astype(jnp.int32)
    places = EXPERTS * 4 * CAP
    place = iota((1, places), 1)
    expert = place // (4 * CAP)
    chosen = jnp.where((first == expert) | (second == expert), 1.0, 0.0)
    r, c = iota((half, half), 0), iota((half, half), 1)
    earlier = jnp.where((r // RB == c // RB) & (c < r), 1.0, 0.0).astype(bf16)
    slot = jnp.dot(earlier, chosen.astype(bf16), preferred_element_type=f32)
    block = iota((half, 1), 0) // RB
    here = (slot == (place % CAP).astype(f32)) & (block == place // CAP % 4)
    table = jnp.transpose(jnp.where(here, chosen, 0.0)).astype(bf16)
    routed = jnp.dot(table, rows, preferred_element_type=f32).astype(bf16)
    for e in range(EXPERTS):
        piece = routed[e * 4 * CAP : (e + 1) * 4 * CAP]
        out_ref[2 * e] = piece
        out_ref[2 * e + 1] = piece


def stage(in_ref, x_ref, feature_ref):
    groups, rows, _ = in_ref.shape
    low_lane = iota((rows, 128), 1) < 64
    feature = jnp.zeros((rows, 128), f32)
    for i in range(groups // 2):
        b_even = in_ref[2 * i, :, 128:].astype(f32)
        b_odd = in_ref[2 * i + 1, :, :128].astype(f32)
        feature = feature + jnp.where(low_lane, b_odd, b_even)
        x_ref[:, 384 * i : 384 * i + 128] = in_ref[2 * i, :, :128]
        x_ref[:, 384 * i + 128 : 384 * i + 256] = jnp.where(low_lane, b_even, b_odd).astype(bf16)
        x_ref[:, 384 * i + 256 : 384 * i + 384] = in_ref[2 * i + 1, :, 128:]
    feature_ref[...] = feature


def experts(x_ref, feature_ref, other_ref, gate_ref, up_ref, down_ref, keep_ref, give_ref, x2_ref, feature2_ref):
    rows = x_ref.shape[0]
    stage(other_ref, x2_ref, feature2_ref)
    feature = jnp.concatenate([feature_ref[...], feature2_ref[...]], axis=0)
    scale = lax.rsqrt(jnp.sum(jnp.transpose(feature), axis=0, keepdims=True) / D + epsilon)
    gate = jnp.zeros((gate_ref.shape[0], 2 * rows), f32)
    up = gate
    for n in range(DEEP):
        part = slice(n * D // DEEP, (n + 1) * D // DEEP)
        x = jnp.concatenate([x_ref[:, part], x2_ref[:, part]], axis=0)
        gate = gate + lax.dot_general(gate_ref[:, part], x, MINOR, preferred_element_type=f32)
        up = up + lax.dot_general(up_ref[:, part], x, MINOR, preferred_element_type=f32)
    gate, up = scale * gate, scale * up
    hidden = jnp.transpose(gate * jax.nn.sigmoid(gate) * up).astype(bf16)
    for n in range(WIDE):
        part = slice(n * D // WIDE, (n + 1) * D // WIDE)
        chunk = jnp.dot(hidden, down_ref[:, part], preferred_element_type=f32)
        keep_ref[:, part] = chunk[:rows]
        give_ref[:, part] = chunk[rows:].astype(bf16)


def spread(keep_ref, other_ref, out_ref):
    for i in range(D // 384):
        a, b, c = (
            keep_ref[:, 128 * n : 128 * n + 128] + other_ref[:, 128 * n : 128 * n + 128].astype(f32)
            for n in range(3 * i, 3 * i + 3)
        )
        for t in range(4):
            rows = slice(t * CAP, (t + 1) * CAP)
            out_ref[(2 * i) * 4 + t] = jnp.concatenate([a[rows], b[rows]], axis=0).astype(bf16)
            out_ref[(2 * i + 1) * 4 + t] = jnp.concatenate([b[rows], c[rows]], axis=0).astype(bf16)


def combiner(routes, weights, out_ref):
    r0, r1 = column(routes[0:1], RB).astype(jnp.int32), column(routes[1:2], RB).astype(jnp.int32)
    w0, w1 = column(weights[0:1], RB), column(weights[1:2], RB)
    place = iota((1, out_ref.shape[1]), 1)
    expert = place // 64
    chosen = jnp.where((r0 == expert) | (r1 == expert), 1.0, 0.0)
    earlier = jnp.where(iota((RB, RB), 1) < iota((RB, RB), 0), 1.0, 0.0)
    slot = jnp.dot(earlier, chosen, preferred_element_type=f32)
    weight = jnp.where(r0 == expert, w0, 0.0) + jnp.where(r1 == expert, w1, 0.0)
    row = (place % 8).astype(f32)
    for part in range(2):
        value = jnp.where(slot + part * CAP == row, weight, 0.0)
        high, rest = halves(value)
        middle, low = halves(rest)
        for n, piece in enumerate((high, middle, low)):
            out_ref[(3 * part + n) * RB : (3 * part + n + 1) * RB, :] = piece.astype(bf16)


def combine(x_ref, table_ref, own_ref, out_ref):
    odd = lax.rem(lax.axis_index("grp"), 2)
    width = out_ref.shape[1]
    x = x_ref[...].reshape(-1, 128)
    both = jnp.dot(table_ref[...], x, preferred_element_type=f32)
    a = both[2 * RB : 3 * RB] + both[RB : 2 * RB] + both[:RB]
    b = both[5 * RB :] + both[4 * RB : 5 * RB] + both[3 * RB : 4 * RB]
    mixture = jnp.concatenate([a, b], axis=1)
    mixture = jnp.where(odd == 1, pltpu.roll(mixture, width, 1), mixture)
    out_ref[...] = (own_ref[...] + mixture)[:, :width].astype(bf16)


def far(x):
    return pltpu.with_memory_space_constraint(x, pltpu.HBM)


def call(kernel, outs, specs, args, scratch=(), flops=0, moved=0, limit=8):
    single = not isinstance(outs, list)
    made = pl.pallas_call(
        kernel,
        out_shape=outs if single else tuple(outs),
        in_specs=specs,
        out_specs=VM if single else tuple(VM for _ in outs),
        scratch_shapes=list(scratch),
        compiler_params=pltpu.CompilerParams(vmem_limit_bytes=limit * 1024 * 1024),
        cost_estimate=pl.CostEstimate(flops=flops, bytes_accessed=moved, transcendentals=0),
    )
    return made(*args)


def shape(dims, dtype):
    return jax.ShapeDtypeStruct(dims, dtype)


def body(
    queries,
    new_keys,
    new_values,
    kv_memory,
    decay_rate,
    attn_gain,
    w_out,
    residual,
    moe_gain,
    w_gate,
    w_up,
    w_down,
    routes,
    route_weights,
):
    groups = lax.axis_size("grp")
    width = residual.shape[1]
    sessions, heads = queries.shape[:2]
    half = groups * sessions // 2
    turned_routes = routes.T
    swap = [(0, 1), (1, 0)]

    decay, narrow, w_turned = decay_rate.reshape(1, -1), moe_gain.reshape(1, -1), w_out.T
    taken = (queries, new_keys, new_values, kv_memory, decay, attn_gain, w_turned, residual, narrow, turned_routes, route_weights.T)
    held = (queries, new_keys, new_values, kv_memory, decay, residual, turned_routes, route_weights.T, narrow)
    taken = tuple(far(x) for x in taken)
    sent, w_near, gain_near, own_rows, moe_near, table = call(
        attention,
        [
            shape((groups, sessions * heads, HEAD_DIM), bf16),
            shape(w_turned.shape, bf16),
            shape(attn_gain.shape, f32),
            shape((RB, LANES), bf16),
            shape((1, LANES), f32),
            shape((6 * RB, 1024), bf16),
        ],
        [HB] * len(taken),
        taken,
        scratch=[pltpu.VMEM(x.shape, x.dtype) for x in held] + [pltpu.SemaphoreType.DMA((10 + sessions,))],
        flops=10**6,
        moved=1200000,
    )
    every = lax.all_to_all(sent, "grp", 0, 0, tiled=True)
    mine, give = call(
        project,
        [shape((half, LANES), f32)] * 2,
        [VM] * 3,
        (every, w_near, gain_near),
        scratch=[pltpu.VMEM((groups * sessions * heads, HEAD_DIM), f32)],
        flops=25 * 10**6,
        moved=700000,
    )
    message, summed = call(
        functools.partial(gather_side, width),
        [shape((half + RB, LANES), bf16), shape((half, LANES), f32)],
        [VM] * 3,
        (mine, lax.ppermute(give, "side", swap), own_rows),
        flops=10**6,
        moved=400000,
    )
    got = [lax.ppermute(message, "tp", [(t, (t + step) % 4) for t in range(4)]) for step in STEPS]
    outbox, own_hidden = call(
        functools.partial(dispatch, width),
        [shape((groups, 4 * CAP, LANES), bf16), shape((RB, LANES), f32)],
        [VM] * 6,
        (summed, own_rows, *got, moe_near),
        scratch=[pltpu.VMEM((half, LANES), f32)] * 2,
        flops=3 * 10**10,
        moved=700000,
    )
    inbox = lax.all_to_all(outbox, "grp", 0, 0, tiled=True)
    staged = [shape((4 * CAP, D), bf16), shape((4 * CAP, 128), f32)]
    x_mine, feature = call(stage, staged, [VM], (inbox,), flops=10**6, moved=500000)
    keep, give = call(
        experts,
        [shape((4 * CAP, D), f32), shape((4 * CAP, D), bf16)],
        [VM] * 6,
        (x_mine, feature, lax.ppermute(inbox, "side", swap), w_gate[0].T, w_up[0].T, w_down[0]),
        scratch=[pltpu.VMEM(x.shape, x.dtype) for x in staged],
        flops=4 * 10**8,
        moved=11000000,
        limit=12,
    )
    back = call(
        spread,
        shape((groups * 4, 2 * CAP, 128), bf16),
        [VM, VM],
        (keep, lax.ppermute(give, "side", swap)),
        flops=10**6,
        moved=900000,
    )
    returned = lax.all_to_all(back, ("grp", "tp"), 0, 0, tiled=True)
    return call(
        combine,
        shape((RB, width), bf16),
        [VM] * 3,
        (returned, table, own_hidden),
        flops=3 * 10**7,
        moved=500000,
    )


def solution(mesh):
    placed = (
        P("grp", ("side", "tp"), None),
        P("grp", ("side", "tp"), None),
        P("grp", ("side", "tp"), None),
        P("grp", ("side", "tp"), None, None),
        P(("side", "tp")),
        P(("side", "tp"), None),
        P(("side", "tp"), "grp"),
        P(("side", "tp"), "grp"),
        P("grp"),
        P("grp", None, ("side", "tp")),
        P("grp", None, ("side", "tp")),
        P("grp", ("side", "tp"), None),
        P(("side", "tp"), None),
        P(("side", "tp"), None),
    )
    return jax.shard_map(
        body, mesh=mesh, in_specs=placed, out_specs=P(("side", "tp"), "grp"), check_vma=False
    )
```

```python
import functools
import jax
import jax.numpy as jnp
from jax import lax
from jax.experimental import pallas as pl
from jax.experimental.pallas import tpu as pltpu
from jax.sharding import PartitionSpec as P

D = 6144
HEADS = 32
HEAD_DIM = 128
EXPERTS = 16
CAP = 4
RB = 16
LANES = 256
DEEP = 6
WIDE = 8

STEPS = (1, 3, 2)
BACK = (2, 3, 1)

epsilon = 1e-06
f32, bf16 = jnp.float32, jnp.bfloat16
VM = pl.BlockSpec(memory_space=pltpu.VMEM)
HB = pl.BlockSpec(memory_space=pltpu.HBM)
MINOR = (((1,), (1,)), ((), ()))


def iota(shape, dim):
    return lax.broadcasted_iota(jnp.int32, shape, dim)


def column(row, size):
    full = jnp.broadcast_to(row, (size, size))
    return jnp.sum(jnp.where(iota((size, size), 0) == iota((size, size), 1), full, 0.0), axis=1, keepdims=True)


def halves(value):
    high = value.astype(bf16).astype(f32)
    return high, value - high


def attention(
    q_hbm, k_hbm, v_hbm, decay_hbm, gain_hbm, kv_hbm, w_hbm, residual_hbm, moe_hbm, routes_hbm, weights_hbm,
    out_ref, gain_ref, w_ref, residual_ref, moe_ref, routes_ref, weights_ref,
    q_ref, k_ref, v_ref, decay_ref, kv_ref, sems,
):
    sessions, heads = q_ref.shape[:2]
    pairs = [(q_hbm, q_ref), (k_hbm, k_ref), (v_hbm, v_ref), (decay_hbm, decay_ref), (gain_hbm, gain_ref)]
    pairs += [(kv_hbm.at[s], kv_ref.at[s]) for s in range(sessions)]
    pairs += [(w_hbm, w_ref), (residual_hbm, residual_ref), (moe_hbm, moe_ref)]
    pairs += [(routes_hbm, routes_ref), (weights_hbm, weights_ref)]
    copies = [pltpu.make_async_copy(source, target, sems.at[i]) for i, (source, target) in enumerate(pairs)]
    for copy in copies:
        copy.start()
    for copy in copies[:5]:
        copy.wait()
    query = jnp.concatenate([q_ref[s].astype(f32) for s in range(sessions)], axis=0)
    key = jnp.concatenate([k_ref[s].astype(f32) for s in range(sessions)], axis=0)
    value = jnp.concatenate([v_ref[s].astype(f32) for s in range(sessions)], axis=0)
    dots = jnp.sum(query * key, axis=1, keepdims=True)
    count = sessions * heads
    ones = jnp.where(iota((count, count * HEAD_DIM), 1) // HEAD_DIM == iota((count, count * HEAD_DIM), 0), 1.0, 0.0)
    turned = jnp.dot(jnp.transpose(query).astype(bf16), ones.astype(bf16), preferred_element_type=f32)
    rows = []
    for s in range(sessions):
        copies[5 + s].wait()
        for h in range(heads):
            n = s * heads + h
            read = jnp.sum(turned[:, n * HEAD_DIM : (n + 1) * HEAD_DIM] * kv_ref[s, h], axis=0, keepdims=True)
            rows.append(decay_ref[:, h : h + 1] * read)
    attended = jnp.concatenate(rows, axis=0) + dots * value
    gain = jnp.concatenate([gain_ref[...]] * sessions, axis=0)
    message = (attended * gain).astype(bf16)
    for g in range(out_ref.shape[0]):
        out_ref[g] = message
    for copy in copies[5 + sessions :]:
        copy.wait()


def prepare(after_ref, residual_ref, moe_ref, routes_ref, weights_ref, own_ref, gain_ref, table_ref):
    width = residual_ref.shape[1]
    routes = routes_ref[...].astype(f32)
    lane = iota((1, LANES), 1)
    own = jnp.concatenate([residual_ref[...].astype(f32), jnp.zeros((RB, LANES - width), f32)], axis=1)
    own = jnp.where(lane == width, column(routes[0:1], RB), jnp.where(lane == width + 1, column(routes[1:2], RB), own))
    own_ref[...] = own.astype(bf16)
    gain_ref[...] = jnp.concatenate([moe_ref[...], jnp.zeros((1, LANES - width), f32)], axis=1)
    combiner(routes, weights_ref[...], table_ref)


def project(x_ref, w_ref, gain_ref, mine_ref, other_ref, spread_ref):
    heads = gain_ref.shape[0]
    width = w_ref.shape[0]
    total = x_ref.shape[0] * x_ref.shape[1]
    sessions = total // heads
    half = sessions // 2
    spread_ref[...] = x_ref[...].reshape(total, HEAD_DIM).astype(f32)
    lane = iota((1, LANES), 1)
    squares = jnp.zeros((sessions, 1), f32)
    parts = []
    for h in range(heads):
        x = spread_ref[pl.ds(h, sessions, stride=heads), :]
        plain = x / gain_ref[h : h + 1, :]
        squares = squares + jnp.sum(plain * plain, axis=1, keepdims=True)
        parts.append(x.astype(bf16))
    projected = lax.dot_general(jnp.concatenate(parts, axis=1), w_ref[...], MINOR, preferred_element_type=f32)
    table = jnp.concatenate([projected, jnp.zeros((sessions, LANES - width), f32)], axis=1)
    table = jnp.where(lane == width, squares, table)
    first = lax.axis_index("side") == 0
    mine_ref[...] = jnp.where(first, table[:half], table[half:])
    other_ref[...] = jnp.where(first, table[half:], table[:half])


def gather_side(width, mine_ref, other_ref, own_ref, out_ref, sum_ref):
    half = mine_ref.shape[0]
    lane = iota((1, LANES), 1)
    table = mine_ref[...] + other_ref[...]
    sum_ref[...] = table
    squares = jnp.sum(jnp.where(lane == width, table, 0.0), axis=1, keepdims=True)
    high, low = halves(squares)
    table = jnp.where(lane == width, high, jnp.where(lane == width + 1, low, table)).astype(bf16)
    out_ref[:half, :] = table
    out_ref[half:, :] = own_ref[...]


def dispatch(width, sum_ref, mine_ref, a_ref, b_ref, c_ref, gain_ref, out_ref, own_ref, rest_ref, scratch_ref):
    half = sum_ref.shape[0]
    tp, odd = lax.axis_index("tp"), lax.rem(lax.axis_index("grp"), 2)
    lane = iota((1, LANES), 1)
    summed = sum_ref[...]
    rest_ref[pl.ds(pl.multiple_of(tp * RB, RB), RB), :] = mine_ref[...].astype(f32)
    for step, ref in zip(STEPS, (a_ref, b_ref, c_ref)):
        summed = summed + ref[:half, :].astype(f32)
        source = lax.rem(tp + 4 - step, 4)
        rest_ref[pl.ds(pl.multiple_of(source * RB, RB), RB), :] = ref[half:, :].astype(f32)
    squares = jnp.sum(jnp.where((lane == width) | (lane == width + 1), summed, 0.0), axis=1, keepdims=True)
    rest = rest_ref[...]
    hidden = jnp.where(lane < width, rest + lax.rsqrt(squares / (HEADS * HEAD_DIM) + epsilon) * summed, 0.0)
    scratch_ref[...] = hidden
    own_ref[...] = scratch_ref[pl.ds(pl.multiple_of(tp * RB, RB), RB), :]
    high, low = halves(jnp.sum(hidden * hidden, axis=1, keepdims=True))
    rows = jnp.where(lane == width, high, jnp.where(lane == width + 1, low, hidden * gain_ref[...]))
    rows = jnp.where(odd == 1, pltpu.roll(rows, LANES - width, 1), rows).astype(bf16)

    first = jnp.sum(jnp.where(lane == width, rest, 0.0), axis=1, keepdims=True).astype(jnp.int32)
    second = jnp.sum(jnp.where(lane == width + 1, rest, 0.0), axis=1, keepdims=True).astype(jnp.int32)
    places = EXPERTS * 4 * CAP
    place = iota((1, places), 1)
    expert = place // (4 * CAP)
    chosen = jnp.where((first == expert) | (second == expert), 1.0, 0.0)
    r, c = iota((half, half), 0), iota((half, half), 1)
    earlier = jnp.where((r // RB == c // RB) & (c < r), 1.0, 0.0).astype(bf16)
    slot = jnp.dot(earlier, chosen.astype(bf16), preferred_element_type=f32)
    block = iota((half, 1), 0) // RB
    here = (slot == (place % CAP).astype(f32)) & (block == place // CAP % 4)
    table = jnp.transpose(jnp.where(here, chosen, 0.0)).astype(bf16)
    routed = jnp.dot(table, rows, preferred_element_type=f32).astype(bf16)
    for e in range(EXPERTS):
        piece = routed[e * 4 * CAP : (e + 1) * 4 * CAP]
        out_ref[2 * e] = piece
        out_ref[2 * e + 1] = piece


def stage(in_ref, x_ref, feature_ref):
    groups, rows, _ = in_ref.shape
    low_lane = iota((rows, 128), 1) < 64
    feature = jnp.zeros((rows, 128), f32)
    for i in range(groups // 2):
        b_even = in_ref[2 * i, :, 128:].astype(f32)
        b_odd = in_ref[2 * i + 1, :, :128].astype(f32)
        feature = feature + jnp.where(low_lane, b_odd, b_even)
        x_ref[:, 384 * i : 384 * i + 128] = in_ref[2 * i, :, :128]
        x_ref[:, 384 * i + 128 : 384 * i + 256] = jnp.where(low_lane, b_even, b_odd).astype(bf16)
        x_ref[:, 384 * i + 256 : 384 * i + 384] = in_ref[2 * i + 1, :, 128:]
    feature_ref[...] = feature


def experts(x_ref, feature_ref, other_ref, gate_ref, up_ref, down_ref, keep_ref, give_ref, x2_ref, feature2_ref):
    rows = x_ref.shape[0]
    stage(other_ref, x2_ref, feature2_ref)
    feature = jnp.concatenate([feature_ref[...], feature2_ref[...]], axis=0)
    scale = lax.rsqrt(jnp.sum(jnp.transpose(feature), axis=0, keepdims=True) / D + epsilon)
    gate = jnp.zeros((gate_ref.shape[0], 2 * rows), f32)
    up = gate
    for n in range(DEEP):
        part = slice(n * D // DEEP, (n + 1) * D // DEEP)
        x = jnp.concatenate([x_ref[:, part], x2_ref[:, part]], axis=0)
        gate = gate + lax.dot_general(gate_ref[:, part], x, MINOR, preferred_element_type=f32)
        up = up + lax.dot_general(up_ref[:, part], x, MINOR, preferred_element_type=f32)
    gate, up = scale * gate, scale * up
    hidden = jnp.transpose(gate * jax.nn.sigmoid(gate) * up).astype(bf16)
    for n in range(WIDE):
        part = slice(n * D // WIDE, (n + 1) * D // WIDE)
        chunk = jnp.dot(hidden, down_ref[:, part], preferred_element_type=f32)
        keep_ref[:, part] = chunk[:rows]
        give_ref[:, part] = chunk[rows:].astype(bf16)


def spread(keep_ref, other_ref, mine_ref, a_ref, b_ref, c_ref, total_ref):
    tp = lax.axis_index("tp")
    for n in range(WIDE):
        part = slice(n * D // WIDE, (n + 1) * D // WIDE)
        total = keep_ref[:, part] + other_ref[:, part].astype(f32)
        for t in range(4):
            total_ref[t, :, part] = total[t * CAP : (t + 1) * CAP]
    span = mine_ref.shape[1]
    for step, ref in zip((0,) + BACK, (mine_ref, a_ref, b_ref, c_ref)):
        rows = total_ref[lax.rem(tp + step, 4)]
        piece = jnp.concatenate([rows[:, q * span : (q + 1) * span] for q in range(4)], axis=0)
        ref[...] = piece.astype(ref.dtype)


def reduce_parts(mine_ref, a_ref, b_ref, c_ref, out_ref):
    total = mine_ref[...]
    for ref in (a_ref, b_ref, c_ref):
        total = total + ref[...].astype(f32)
    for q in range(4):
        rows = total[q * CAP : (q + 1) * CAP]
        for i in range(4):
            a, b, c = (rows[:, 384 * i + 128 * n : 384 * i + 128 * (n + 1)] for n in range(3))
            out_ref[q * 8 + 2 * i] = jnp.concatenate([a, b], axis=0).astype(out_ref.dtype)
            out_ref[q * 8 + 2 * i + 1] = jnp.concatenate([b, c], axis=0).astype(out_ref.dtype)


def combiner(routes, weights, out_ref):
    r0, r1 = column(routes[0:1], RB).astype(jnp.int32), column(routes[1:2], RB).astype(jnp.int32)
    w0, w1 = column(weights[0:1], RB), column(weights[1:2], RB)
    place = iota((1, out_ref.shape[1]), 1)
    expert = place // 16
    chosen = jnp.where((r0 == expert) | (r1 == expert), 1.0, 0.0)
    earlier = jnp.where(iota((RB, RB), 1) < iota((RB, RB), 0), 1.0, 0.0)
    slot = jnp.dot(earlier, chosen, preferred_element_type=f32)
    weight = jnp.where(r0 == expert, w0, 0.0) + jnp.where(r1 == expert, w1, 0.0)
    row = (place % 8).astype(f32)
    for part in range(2):
        value = jnp.where(slot + part * CAP == row, weight, 0.0)
        high, rest = halves(value)
        middle, low = halves(rest)
        for n, piece in enumerate((high, middle, low)):
            out_ref[(3 * part + n) * RB : (3 * part + n + 1) * RB, :] = piece.astype(bf16)


def combine(x_ref, table_ref, own_ref, out_ref):
    odd = lax.rem(lax.axis_index("grp"), 2)
    width = out_ref.shape[1]
    x = x_ref[...].reshape(-1, 128)
    both = jnp.dot(table_ref[...], x, preferred_element_type=f32)
    a = both[2 * RB : 3 * RB] + both[RB : 2 * RB] + both[:RB]
    b = both[5 * RB :] + both[4 * RB : 5 * RB] + both[3 * RB : 4 * RB]
    mixture = jnp.concatenate([a, b], axis=1)
    mixture = jnp.where(odd == 1, pltpu.roll(mixture, width, 1), mixture)
    out_ref[...] = (own_ref[...] + mixture)[:, :width].astype(bf16)


def far(x):
    return pltpu.with_memory_space_constraint(x, pltpu.HBM)


def call(kernel, outs, specs, args, scratch=(), flops=0, moved=0, limit=8):
    single = not isinstance(outs, list)
    made = pl.pallas_call(
        kernel,
        out_shape=outs if single else tuple(outs),
        in_specs=specs,
        out_specs=VM if single else tuple(VM for _ in outs),
        scratch_shapes=list(scratch),
        compiler_params=pltpu.CompilerParams(vmem_limit_bytes=limit * 1024 * 1024),
        cost_estimate=pl.CostEstimate(flops=flops, bytes_accessed=moved, transcendentals=0),
    )
    return made(*args)


def shape(dims, dtype):
    return jax.ShapeDtypeStruct(dims, dtype)


def body(
    queries,
    new_keys,
    new_values,
    kv_memory,
    decay_rate,
    attn_gain,
    w_out,
    residual,
    moe_gain,
    w_gate,
    w_up,
    w_down,
    routes,
    route_weights,
):
    groups = lax.axis_size("grp")
    width = residual.shape[1]
    sessions, heads = queries.shape[:2]
    half = groups * sessions // 2
    turned_routes = routes.T
    swap = [(0, 1), (1, 0)]

    decay, narrow, w_turned = decay_rate.reshape(1, -1), moe_gain.reshape(1, -1), w_out.T
    held = (queries, new_keys, new_values, decay)
    passed = (w_turned, residual, narrow, turned_routes, route_weights.T)
    taken = tuple(far(x) for x in held + (attn_gain, kv_memory) + passed)
    sent, gain_near, w_near, *rest = call(
        attention,
        [shape((groups, sessions * heads, HEAD_DIM), bf16)] + [shape(x.shape, x.dtype) for x in (attn_gain,) + passed],
        [HB] * len(taken),
        taken,
        scratch=[pltpu.VMEM(x.shape, x.dtype) for x in held + (kv_memory,)]
        + [pltpu.SemaphoreType.DMA((10 + sessions,))],
        flops=10**6,
        moved=1200000,
    )
    every = lax.all_to_all(sent, "grp", 0, 0, tiled=True)
    mine, give = call(
        project,
        [shape((half, LANES), f32)] * 2,
        [VM] * 3,
        (every, w_near, gain_near),
        scratch=[pltpu.VMEM((groups * sessions * heads, HEAD_DIM), f32)],
        flops=25 * 10**6,
        moved=700000,
    )
    own_rows, moe_near, table = call(
        prepare,
        [shape((RB, LANES), bf16), shape((1, LANES), f32), shape((6 * RB, 256), bf16)],
        [VM] * 5,
        (give, *rest),
        flops=10**6,
        moved=200000,
    )
    message, summed = call(
        functools.partial(gather_side, width),
        [shape((half + RB, LANES), bf16), shape((half, LANES), f32)],
        [VM] * 3,
        (mine, lax.ppermute(give, "side", swap), own_rows),
        flops=3 * 10**10,
        moved=400000,
    )
    got = [lax.ppermute(message, "tp", [(t, (t + step) % 4) for t in range(4)]) for step in STEPS]
    outbox, own_hidden = call(
        functools.partial(dispatch, width),
        [shape((groups, 4 * CAP, LANES), bf16), shape((RB, LANES), f32)],
        [VM] * 6,
        (summed, own_rows, *got, moe_near),
        scratch=[pltpu.VMEM((half, LANES), f32)] * 2,
        flops=10**7,
        moved=700000,
    )
    inbox = lax.all_to_all(outbox, "grp", 0, 0, tiled=True)
    staged = [shape((4 * CAP, D), bf16), shape((4 * CAP, 128), f32)]
    x_mine, feature = call(stage, staged, [VM], (inbox,), flops=10**6, moved=500000)
    keep, give = call(
        experts,
        [shape((4 * CAP, D), f32), shape((4 * CAP, D), bf16)],
        [VM] * 6,
        (x_mine, feature, lax.ppermute(inbox, "side", swap), w_gate[0].T, w_up[0].T, w_down[0]),
        scratch=[pltpu.VMEM(x.shape, x.dtype) for x in staged],
        flops=4 * 10**8,
        moved=11000000,
        limit=12,
    )
    piece = (4 * CAP, D // 4)
    sums, *pieces = call(
        spread,
        [shape(piece, f32)] + [shape(piece, bf16)] * 3,
        [VM, VM],
        (keep, lax.ppermute(give, "side", swap)),
        scratch=[pltpu.VMEM((4, CAP, D), f32)],
        flops=10**6,
        moved=900000,
    )
    pieces = [lax.ppermute(x, "tp", [(t, (t + step) % 4) for t in range(4)]) for step, x in zip(BACK, pieces)]
    back = call(
        reduce_parts,
        shape((groups, 2 * CAP, 128), bf16),
        [VM] * 4,
        (sums, *pieces),
        flops=10**6,
        moved=400000,
    )
    returned = lax.all_to_all(back, "grp", 0, 0, tiled=True)
    return call(
        combine,
        shape((RB, width), bf16),
        [VM] * 3,
        (returned, table, own_hidden),
        flops=3 * 10**7,
        moved=500000,
    )


def solution(mesh):
    placed = (
        P("grp", ("side", "tp"), None),
        P("grp", ("side", "tp"), None),
        P("grp", ("side", "tp"), None),
        P("grp", ("side", "tp"), None, None),
        P(("side", "tp")),
        P(("side", "tp"), None),
        P(("side", "tp"), "grp"),
        P(("side", "tp"), "grp"),
        P("grp"),
        P("grp", None, ("side", "tp")),
        P("grp", None, ("side", "tp")),
        P("grp", ("side", "tp"), None),
        P(("side", "tp"), None),
        P(("side", "tp"), None),
    )
    return jax.shard_map(
        body, mesh=mesh, in_specs=placed, out_specs=P(("side", "tp"), "grp"), check_vma=False
    )
```

```python
import functools
import jax
import jax.numpy as jnp
from jax import lax
from jax.experimental import pallas as pl
from jax.experimental.pallas import tpu as pltpu
from jax.sharding import PartitionSpec as P

D = 6144
HEADS = 32
HEAD_DIM = 128
EXPERTS = 16
CAP = 4
RB = 16
LANES = 256
DEEP = 6
WIDE = 8

STEPS = (1, 3, 2)

epsilon = 1e-06
f32, bf16 = jnp.float32, jnp.bfloat16
VM = pl.BlockSpec(memory_space=pltpu.VMEM)
HB = pl.BlockSpec(memory_space=pltpu.HBM)
MINOR = (((1,), (1,)), ((), ()))


def iota(shape, dim):
    return lax.broadcasted_iota(jnp.int32, shape, dim)


def column(row, size):
    full = jnp.broadcast_to(row, (size, size))
    return jnp.sum(jnp.where(iota((size, size), 0) == iota((size, size), 1), full, 0.0), axis=1, keepdims=True)


def halves(value):
    high = value.astype(bf16).astype(f32)
    return high, value - high


def attention(
    q_hbm, k_hbm, v_hbm, decay_hbm, gain_hbm, kv_hbm, w_hbm, residual_hbm, moe_hbm, routes_hbm, weights_hbm,
    out_ref, gain_ref, w_ref, residual_ref, moe_ref, routes_ref, weights_ref,
    q_ref, k_ref, v_ref, decay_ref, kv_ref, sems,
):
    sessions, heads = q_ref.shape[:2]
    pairs = [(q_hbm, q_ref), (k_hbm, k_ref), (v_hbm, v_ref), (decay_hbm, decay_ref), (gain_hbm, gain_ref)]
    pairs += [(kv_hbm.at[s], kv_ref.at[s]) for s in range(sessions)]
    pairs += [(w_hbm, w_ref), (residual_hbm, residual_ref), (moe_hbm, moe_ref)]
    pairs += [(routes_hbm, routes_ref), (weights_hbm, weights_ref)]
    copies = [pltpu.make_async_copy(source, target, sems.at[i]) for i, (source, target) in enumerate(pairs)]
    for copy in copies:
        copy.start()
    for copy in copies[:5]:
        copy.wait()
    query = jnp.concatenate([q_ref[s].astype(f32) for s in range(sessions)], axis=0)
    key = jnp.concatenate([k_ref[s].astype(f32) for s in range(sessions)], axis=0)
    value = jnp.concatenate([v_ref[s].astype(f32) for s in range(sessions)], axis=0)
    dots = jnp.sum(query * key, axis=1, keepdims=True)
    count = sessions * heads
    ones = jnp.where(iota((count, count * HEAD_DIM), 1) // HEAD_DIM == iota((count, count * HEAD_DIM), 0), 1.0, 0.0)
    turned = jnp.dot(jnp.transpose(query).astype(bf16), ones.astype(bf16), preferred_element_type=f32)
    rows = []
    for s in range(sessions):
        copies[5 + s].wait()
        for h in range(heads):
            n = s * heads + h
            read = jnp.sum(turned[:, n * HEAD_DIM : (n + 1) * HEAD_DIM] * kv_ref[s, h], axis=0, keepdims=True)
            rows.append(decay_ref[:, h : h + 1] * read)
    attended = jnp.concatenate(rows, axis=0) + dots * value
    gain = jnp.concatenate([gain_ref[...]] * sessions, axis=0)
    message = (attended * gain).astype(bf16)
    for g in range(out_ref.shape[0]):
        out_ref[g] = message
    for copy in copies[5 + sessions :]:
        copy.wait()


def prepare(after_ref, residual_ref, moe_ref, routes_ref, weights_ref, own_ref, gain_ref, table_ref):
    width = residual_ref.shape[1]
    routes = routes_ref[...].astype(f32)
    lane = iota((1, LANES), 1)
    own = jnp.concatenate([residual_ref[...].astype(f32), jnp.zeros((RB, LANES - width), f32)], axis=1)
    own = jnp.where(lane == width, column(routes[0:1], RB), jnp.where(lane == width + 1, column(routes[1:2], RB), own))
    own_ref[...] = own.astype(bf16)
    gain_ref[...] = jnp.concatenate([moe_ref[...], jnp.zeros((1, LANES - width), f32)], axis=1)
    combiner(routes, weights_ref[...], table_ref)


def project(x_ref, w_ref, gain_ref, mine_ref, other_ref, spread_ref):
    heads = gain_ref.shape[0]
    width = w_ref.shape[0]
    total = x_ref.shape[0] * x_ref.shape[1]
    sessions = total // heads
    half = sessions // 2
    spread_ref[:total] = x_ref[...].reshape(total, HEAD_DIM).astype(f32)
    lane = iota((1, LANES), 1)
    squares = jnp.zeros((sessions, 1), f32)
    parts = []
    for h in range(heads):
        x = spread_ref[pl.ds(h, sessions, stride=heads), :]
        plain = x / gain_ref[h : h + 1, :]
        squares = squares + jnp.sum(plain * plain, axis=1, keepdims=True)
        parts.append(x.astype(bf16))
    projected = lax.dot_general(jnp.concatenate(parts, axis=1), w_ref[...], MINOR, preferred_element_type=f32)
    table = jnp.concatenate([projected, jnp.zeros((sessions, LANES - width), f32)], axis=1)
    table = jnp.where(lane == width, squares, table)
    first = lax.axis_index("side") == 0
    mine_ref[...] = jnp.where(first, table[:half], table[half:])
    other_ref[...] = jnp.where(first, table[half:], table[:half])


def gather_side(width, mine_ref, other_ref, own_ref, out_ref, sum_ref):
    half = mine_ref.shape[0]
    lane = iota((1, LANES), 1)
    table = mine_ref[...] + other_ref[...]
    sum_ref[...] = table
    squares = jnp.sum(jnp.where(lane == width, table, 0.0), axis=1, keepdims=True)
    high, low = halves(squares)
    table = jnp.where(lane == width, high, jnp.where(lane == width + 1, low, table)).astype(bf16)
    out_ref[:half, :] = table
    out_ref[half:, :] = own_ref[...]


def dispatch(width, sum_ref, mine_ref, a_ref, b_ref, c_ref, gain_ref, out_ref, own_ref, rest_ref, scratch_ref):
    half = sum_ref.shape[0]
    tp, odd = lax.axis_index("tp"), lax.rem(lax.axis_index("grp"), 2)
    lane = iota((1, LANES), 1)
    summed = sum_ref[...]
    rest_ref[pl.ds(pl.multiple_of(tp * RB, RB), RB), :] = mine_ref[...].astype(f32)
    for step, ref in zip(STEPS, (a_ref, b_ref, c_ref)):
        summed = summed + ref[:half, :].astype(f32)
        source = lax.rem(tp + 4 - step, 4)
        rest_ref[pl.ds(pl.multiple_of(source * RB, RB), RB), :] = ref[half:, :].astype(f32)
    squares = jnp.sum(jnp.where((lane == width) | (lane == width + 1), summed, 0.0), axis=1, keepdims=True)
    rest = rest_ref[...]
    hidden = jnp.where(lane < width, rest + lax.rsqrt(squares / (HEADS * HEAD_DIM) + epsilon) * summed, 0.0)
    scratch_ref[...] = hidden
    own_ref[...] = scratch_ref[pl.ds(pl.multiple_of(tp * RB, RB), RB), :]
    high, low = halves(jnp.sum(hidden * hidden, axis=1, keepdims=True))
    rows = jnp.where(lane == width, high, jnp.where(lane == width + 1, low, hidden * gain_ref[...]))
    rows = jnp.where(odd == 1, pltpu.roll(rows, LANES - width, 1), rows).astype(bf16)

    first = jnp.sum(jnp.where(lane == width, rest, 0.0), axis=1, keepdims=True).astype(jnp.int32)
    second = jnp.sum(jnp.where(lane == width + 1, rest, 0.0), axis=1, keepdims=True).astype(jnp.int32)
    places = EXPERTS * 4 * CAP
    place = iota((1, places), 1)
    expert = place // (4 * CAP)
    chosen = jnp.where((first == expert) | (second == expert), 1.0, 0.0)
    r, c = iota((half, half), 0), iota((half, half), 1)
    earlier = jnp.where((r // RB == c // RB) & (c < r), 1.0, 0.0).astype(bf16)
    slot = jnp.dot(earlier, chosen.astype(bf16), preferred_element_type=f32)
    block = iota((half, 1), 0) // RB
    here = (slot == (place % CAP).astype(f32)) & (block == place // CAP % 4)
    table = jnp.transpose(jnp.where(here, chosen, 0.0)).astype(bf16)
    routed = jnp.dot(table, rows, preferred_element_type=f32).astype(bf16)
    for e in range(EXPERTS):
        piece = routed[e * 4 * CAP : (e + 1) * 4 * CAP]
        out_ref[2 * e] = piece
        out_ref[2 * e + 1] = piece


def stage(in_ref, x_ref, feature_ref):
    groups, rows, _ = in_ref.shape
    low_lane = iota((rows, 128), 1) < 64
    feature = jnp.zeros((rows, 128), f32)
    for i in range(groups // 2):
        b_even = in_ref[2 * i, :, 128:].astype(f32)
        b_odd = in_ref[2 * i + 1, :, :128].astype(f32)
        feature = feature + jnp.where(low_lane, b_odd, b_even)
        x_ref[:, 384 * i : 384 * i + 128] = in_ref[2 * i, :, :128]
        x_ref[:, 384 * i + 128 : 384 * i + 256] = jnp.where(low_lane, b_even, b_odd).astype(bf16)
        x_ref[:, 384 * i + 256 : 384 * i + 384] = in_ref[2 * i + 1, :, 128:]
    feature_ref[...] = feature


def experts(x_ref, feature_ref, other_ref, gate_ref, up_ref, down_ref, keep_ref, give_ref, x2_ref, feature2_ref):
    rows = x_ref.shape[0]
    stage(other_ref, x2_ref, feature2_ref)
    feature = jnp.concatenate([feature_ref[...], feature2_ref[...]], axis=0)
    scale = lax.rsqrt(jnp.sum(jnp.transpose(feature), axis=0, keepdims=True) / D + epsilon)
    gate = jnp.zeros((gate_ref.shape[0], 2 * rows), f32)
    up = gate
    for n in range(DEEP):
        part = slice(n * D // DEEP, (n + 1) * D // DEEP)
        x = jnp.concatenate([x_ref[:, part], x2_ref[:, part]], axis=0)
        gate = gate + lax.dot_general(gate_ref[:, part], x, MINOR, preferred_element_type=f32)
        up = up + lax.dot_general(up_ref[:, part], x, MINOR, preferred_element_type=f32)
    gate, up = scale * gate, scale * up
    hidden = jnp.transpose(gate * jax.nn.sigmoid(gate) * up).astype(bf16)
    for n in range(WIDE):
        part = slice(n * D // WIDE, (n + 1) * D // WIDE)
        chunk = jnp.dot(hidden, down_ref[:, part], preferred_element_type=f32)
        keep_ref[:, part] = chunk[:rows]
        give_ref[:, part] = chunk[rows:].astype(bf16)


def spread(keep_ref, other_ref, out_ref):
    for i in range(D // 384):
        a, b, c = (
            keep_ref[:, 128 * n : 128 * n + 128] + other_ref[:, 128 * n : 128 * n + 128].astype(f32)
            for n in range(3 * i, 3 * i + 3)
        )
        for t in range(4):
            rows = slice(t * CAP, (t + 1) * CAP)
            out_ref[(2 * i) * 4 + t] = jnp.concatenate([a[rows], b[rows]], axis=0).astype(bf16)
            out_ref[(2 * i + 1) * 4 + t] = jnp.concatenate([b[rows], c[rows]], axis=0).astype(bf16)


def combiner(routes, weights, out_ref):
    r0, r1 = column(routes[0:1], RB).astype(jnp.int32), column(routes[1:2], RB).astype(jnp.int32)
    w0, w1 = column(weights[0:1], RB), column(weights[1:2], RB)
    place = iota((1, out_ref.shape[1]), 1)
    expert = place // 64
    chosen = jnp.where((r0 == expert) | (r1 == expert), 1.0, 0.0)
    earlier = jnp.where(iota((RB, RB), 1) < iota((RB, RB), 0), 1.0, 0.0)
    slot = jnp.dot(earlier, chosen, preferred_element_type=f32)
    weight = jnp.where(r0 == expert, w0, 0.0) + jnp.where(r1 == expert, w1, 0.0)
    row = (place % 8).astype(f32)
    for part in range(2):
        value = jnp.where(slot + part * CAP == row, weight, 0.0)
        high, rest = halves(value)
        middle, low = halves(rest)
        for n, piece in enumerate((high, middle, low)):
            out_ref[(3 * part + n) * RB : (3 * part + n + 1) * RB, :] = piece.astype(bf16)


def combine(x_ref, table_ref, own_ref, out_ref):
    odd = lax.rem(lax.axis_index("grp"), 2)
    width = out_ref.shape[1]
    x = x_ref[...].reshape(-1, 128)
    both = jnp.dot(table_ref[...], x, preferred_element_type=f32)
    a = both[2 * RB : 3 * RB] + both[RB : 2 * RB] + both[:RB]
    b = both[5 * RB :] + both[4 * RB : 5 * RB] + both[3 * RB : 4 * RB]
    mixture = jnp.concatenate([a, b], axis=1)
    mixture = jnp.where(odd == 1, pltpu.roll(mixture, width, 1), mixture)
    out_ref[...] = (own_ref[...] + mixture)[:, :width].astype(bf16)


def far(x):
    return pltpu.with_memory_space_constraint(x, pltpu.HBM)


def call(kernel, outs, specs, args, scratch=(), flops=0, moved=0, limit=8):
    single = not isinstance(outs, list)
    made = pl.pallas_call(
        kernel,
        out_shape=outs if single else tuple(outs),
        in_specs=specs,
        out_specs=VM if single else tuple(VM for _ in outs),
        scratch_shapes=list(scratch),
        compiler_params=pltpu.CompilerParams(vmem_limit_bytes=limit * 1024 * 1024),
        cost_estimate=pl.CostEstimate(flops=flops, bytes_accessed=moved, transcendentals=0),
    )
    return made(*args)


def shape(dims, dtype):
    return jax.ShapeDtypeStruct(dims, dtype)


def body(
    queries,
    new_keys,
    new_values,
    kv_memory,
    decay_rate,
    attn_gain,
    w_out,
    residual,
    moe_gain,
    w_gate,
    w_up,
    w_down,
    routes,
    route_weights,
):
    groups = lax.axis_size("grp")
    width = residual.shape[1]
    sessions, heads = queries.shape[:2]
    half = groups * sessions // 2
    turned_routes = routes.T
    swap = [(0, 1), (1, 0)]

    decay, narrow, w_turned = decay_rate.reshape(1, -1), moe_gain.reshape(1, -1), w_out.T
    held = (queries, new_keys, new_values, decay)
    passed = (w_turned, residual, narrow, turned_routes, route_weights.T)
    taken = tuple(far(x) for x in held + (attn_gain, kv_memory) + passed)
    sent, gain_near, w_near, *rest = call(
        attention,
        [shape((groups, sessions * heads, HEAD_DIM), bf16)] + [shape(x.shape, x.dtype) for x in (attn_gain,) + passed],
        [HB] * len(taken),
        taken,
        scratch=[pltpu.VMEM(x.shape, x.dtype) for x in held + (kv_memory,)]
        + [pltpu.SemaphoreType.DMA((10 + sessions,))],
        flops=10**6,
        moved=1200000,
    )
    every = lax.all_to_all(sent, "grp", 0, 0, tiled=True)
    mine, give = call(
        project,
        [shape((half, LANES), f32)] * 2,
        [VM] * 3,
        (every, w_near, gain_near),
        scratch=[pltpu.VMEM((groups * sessions * heads + 8, HEAD_DIM), f32)],
        flops=25 * 10**6,
        moved=700000,
    )
    own_rows, moe_near, table = call(
        prepare,
        [shape((RB, LANES), bf16), shape((1, LANES), f32), shape((6 * RB, 1024), bf16)],
        [VM] * 5,
        (give, *rest),
        flops=10**6,
        moved=200000,
    )
    message, summed = call(
        functools.partial(gather_side, width),
        [shape((half + RB, LANES), bf16), shape((half, LANES), f32)],
        [VM] * 3,
        (mine, lax.ppermute(give, "side", swap), own_rows),
        flops=3 * 10**10,
        moved=400000,
    )
    got = [lax.ppermute(message, "tp", [(t, (t + step) % 4) for t in range(4)]) for step in STEPS]
    outbox, own_hidden = call(
        functools.partial(dispatch, width),
        [shape((groups, 4 * CAP, LANES), bf16), shape((RB, LANES), f32)],
        [VM] * 6,
        (summed, own_rows, *got, moe_near),
        scratch=[pltpu.VMEM((half, LANES), f32)] * 2,
        flops=10**7,
        moved=700000,
    )
    inbox = lax.all_to_all(outbox, "grp", 0, 0, tiled=True)
    staged = [shape((4 * CAP, D), bf16), shape((4 * CAP, 128), f32)]
    x_mine, feature = call(stage, staged, [VM], (inbox,), flops=10**6, moved=500000)
    keep, give = call(
        experts,
        [shape((4 * CAP, D), f32), shape((4 * CAP, D), bf16)],
        [VM] * 6,
        (x_mine, feature, lax.ppermute(inbox, "side", swap), w_gate[0].T, w_up[0].T, w_down[0]),
        scratch=[pltpu.VMEM(x.shape, x.dtype) for x in staged],
        flops=4 * 10**8,
        moved=11000000,
        limit=12,
    )
    back = call(
        spread,
        shape((groups * 4, 2 * CAP, 128), bf16),
        [VM, VM],
        (keep, lax.ppermute(give, "side", swap)),
        flops=10**6,
        moved=900000,
    )
    returned = lax.all_to_all(back, ("grp", "tp"), 0, 0, tiled=True)
    return call(
        combine,
        shape((RB, width), bf16),
        [VM] * 3,
        (returned, table, own_hidden),
        flops=3 * 10**7,
        moved=500000,
    )


def solution(mesh):
    placed = (
        P("grp", ("side", "tp"), None),
        P("grp", ("side", "tp"), None),
        P("grp", ("side", "tp"), None),
        P("grp", ("side", "tp"), None, None),
        P(("side", "tp")),
        P(("side", "tp"), None),
        P(("side", "tp"), "grp"),
        P(("side", "tp"), "grp"),
        P("grp"),
        P("grp", None, ("side", "tp")),
        P("grp", None, ("side", "tp")),
        P("grp", ("side", "tp"), None),
        P(("side", "tp"), None),
        P(("side", "tp"), None),
    )
    return jax.shard_map(
        body, mesh=mesh, in_specs=placed, out_specs=P(("side", "tp"), "grp"), check_vma=False
    )
```

```python
import functools
import jax
import jax.numpy as jnp
from jax import lax
from jax.experimental import pallas as pl
from jax.experimental.pallas import tpu as pltpu
from jax.sharding import PartitionSpec as P

D = 6144
HEADS = 32
HEAD_DIM = 128
EXPERTS = 16
CAP = 4
RB = 16
LANES = 256
DEEP = 1
WIDE = 8

STEPS = (1, 3, 2)

epsilon = 1e-06
f32, bf16 = jnp.float32, jnp.bfloat16
VM = pl.BlockSpec(memory_space=pltpu.VMEM)
HB = pl.BlockSpec(memory_space=pltpu.HBM)
MINOR = (((1,), (1,)), ((), ()))


def iota(shape, dim):
    return lax.broadcasted_iota(jnp.int32, shape, dim)


def column(row, size):
    full = jnp.broadcast_to(row, (size, size))
    return jnp.sum(jnp.where(iota((size, size), 0) == iota((size, size), 1), full, 0.0), axis=1, keepdims=True)


def halves(value):
    high = value.astype(bf16).astype(f32)
    return high, value - high


def attention(
    q_hbm, k_hbm, v_hbm, decay_hbm, gain_hbm, kv_hbm, w_hbm, residual_hbm, moe_hbm, routes_hbm, weights_hbm,
    out_ref, gain_ref, w_ref, residual_ref, moe_ref, routes_ref, weights_ref,
    q_ref, k_ref, v_ref, decay_ref, kv_ref, sems,
):
    sessions, heads = q_ref.shape[:2]
    pairs = [(q_hbm, q_ref), (k_hbm, k_ref), (v_hbm, v_ref), (decay_hbm, decay_ref), (gain_hbm, gain_ref)]
    pairs += [(kv_hbm.at[s], kv_ref.at[s]) for s in range(sessions)]
    pairs += [(w_hbm, w_ref), (residual_hbm, residual_ref), (moe_hbm, moe_ref)]
    pairs += [(routes_hbm, routes_ref), (weights_hbm, weights_ref)]
    copies = [pltpu.make_async_copy(source, target, sems.at[i]) for i, (source, target) in enumerate(pairs)]
    for copy in copies:
        copy.start()
    for copy in copies[:5]:
        copy.wait()
    query = jnp.concatenate([q_ref[s].astype(f32) for s in range(sessions)], axis=0)
    key = jnp.concatenate([k_ref[s].astype(f32) for s in range(sessions)], axis=0)
    value = jnp.concatenate([v_ref[s].astype(f32) for s in range(sessions)], axis=0)
    dots = jnp.sum(query * key, axis=1, keepdims=True)
    count = sessions * heads
    ones = jnp.where(iota((count, count * HEAD_DIM), 1) // HEAD_DIM == iota((count, count * HEAD_DIM), 0), 1.0, 0.0)
    turned = jnp.dot(jnp.transpose(query).astype(bf16), ones.astype(bf16), preferred_element_type=f32)
    rows = []
    for s in range(sessions):
        copies[5 + s].wait()
        for h in range(heads):
            n = s * heads + h
            read = jnp.sum(turned[:, n * HEAD_DIM : (n + 1) * HEAD_DIM] * kv_ref[s, h], axis=0, keepdims=True)
            rows.append(decay_ref[:, h : h + 1] * read)
    attended = jnp.concatenate(rows, axis=0) + dots * value
    gain = jnp.concatenate([gain_ref[...]] * sessions, axis=0)
    message = (attended * gain).astype(bf16)
    for g in range(out_ref.shape[0]):
        out_ref[g] = message
    for copy in copies[5 + sessions :]:
        copy.wait()


def prepare(after_ref, residual_ref, moe_ref, routes_ref, weights_ref, own_ref, gain_ref, table_ref):
    width = residual_ref.shape[1]
    routes = routes_ref[...].astype(f32)
    lane = iota((1, LANES), 1)
    own = jnp.concatenate([residual_ref[...].astype(f32), jnp.zeros((RB, LANES - width), f32)], axis=1)
    own = jnp.where(lane == width, column(routes[0:1], RB), jnp.where(lane == width + 1, column(routes[1:2], RB), own))
    own_ref[...] = own.astype(bf16)
    gain_ref[...] = jnp.concatenate([moe_ref[...], jnp.zeros((1, LANES - width), f32)], axis=1)
    combiner(routes, weights_ref[...], table_ref)


def project(x_ref, w_ref, gain_ref, mine_ref, other_ref, spread_ref):
    heads = gain_ref.shape[0]
    width = w_ref.shape[0]
    total = x_ref.shape[0] * x_ref.shape[1]
    sessions = total // heads
    half = sessions // 2
    spread_ref[:total] = x_ref[...].reshape(total, HEAD_DIM).astype(f32)
    lane = iota((1, LANES), 1)
    squares = jnp.zeros((sessions, 1), f32)
    parts = []
    for h in range(heads):
        x = spread_ref[pl.ds(h, sessions, stride=heads), :]
        plain = x / gain_ref[h : h + 1, :]
        squares = squares + jnp.sum(plain * plain, axis=1, keepdims=True)
        parts.append(x.astype(bf16))
    projected = lax.dot_general(jnp.concatenate(parts, axis=1), w_ref[...], MINOR, preferred_element_type=f32)
    table = jnp.concatenate([projected, jnp.zeros((sessions, LANES - width), f32)], axis=1)
    table = jnp.where(lane == width, squares, table)
    first = lax.axis_index("side") == 0
    mine_ref[...] = jnp.where(first, table[:half], table[half:])
    other_ref[...] = jnp.where(first, table[half:], table[:half])


def gather_side(width, mine_ref, other_ref, own_ref, out_ref, sum_ref):
    half = mine_ref.shape[0]
    lane = iota((1, LANES), 1)
    table = mine_ref[...] + other_ref[...]
    sum_ref[...] = table
    squares = jnp.sum(jnp.where(lane == width, table, 0.0), axis=1, keepdims=True)
    high, low = halves(squares)
    table = jnp.where(lane == width, high, jnp.where(lane == width + 1, low, table)).astype(bf16)
    out_ref[:half, :] = table
    out_ref[half:, :] = own_ref[...]


def dispatch(width, sum_ref, mine_ref, a_ref, b_ref, c_ref, gain_ref, out_ref, own_ref, rest_ref, scratch_ref):
    half = sum_ref.shape[0]
    tp, odd = lax.axis_index("tp"), lax.rem(lax.axis_index("grp"), 2)
    lane = iota((1, LANES), 1)
    summed = sum_ref[...]
    rest_ref[pl.ds(pl.multiple_of(tp * RB, RB), RB), :] = mine_ref[...].astype(f32)
    for step, ref in zip(STEPS, (a_ref, b_ref, c_ref)):
        summed = summed + ref[:half, :].astype(f32)
        source = lax.rem(tp + 4 - step, 4)
        rest_ref[pl.ds(pl.multiple_of(source * RB, RB), RB), :] = ref[half:, :].astype(f32)
    squares = jnp.sum(jnp.where((lane == width) | (lane == width + 1), summed, 0.0), axis=1, keepdims=True)
    rest = rest_ref[...]
    hidden = jnp.where(lane < width, rest + lax.rsqrt(squares / (HEADS * HEAD_DIM) + epsilon) * summed, 0.0)
    scratch_ref[...] = hidden
    own_ref[...] = scratch_ref[pl.ds(pl.multiple_of(tp * RB, RB), RB), :]
    high, low = halves(jnp.sum(hidden * hidden, axis=1, keepdims=True))
    rows = jnp.where(lane == width, high, jnp.where(lane == width + 1, low, hidden * gain_ref[...]))
    rows = jnp.where(odd == 1, pltpu.roll(rows, LANES - width, 1), rows).astype(bf16)

    first = jnp.sum(jnp.where(lane == width, rest, 0.0), axis=1, keepdims=True).astype(jnp.int32)
    second = jnp.sum(jnp.where(lane == width + 1, rest, 0.0), axis=1, keepdims=True).astype(jnp.int32)
    places = EXPERTS * 4 * CAP
    place = iota((1, places), 1)
    expert = place // (4 * CAP)
    chosen = jnp.where((first == expert) | (second == expert), 1.0, 0.0)
    r, c = iota((half, half), 0), iota((half, half), 1)
    earlier = jnp.where((r // RB == c // RB) & (c < r), 1.0, 0.0).astype(bf16)
    slot = jnp.dot(earlier, chosen.astype(bf16), preferred_element_type=f32)
    block = iota((half, 1), 0) // RB
    here = (slot == (place % CAP).astype(f32)) & (block == place // CAP % 4)
    table = jnp.transpose(jnp.where(here, chosen, 0.0)).astype(bf16)
    routed = jnp.dot(table, rows, preferred_element_type=f32).astype(bf16)
    for e in range(EXPERTS):
        piece = routed[e * 4 * CAP : (e + 1) * 4 * CAP]
        out_ref[2 * e] = piece
        out_ref[2 * e + 1] = piece


def stage(in_ref, x_ref):
    groups, rows, _ = in_ref.shape
    low_lane = iota((rows, 128), 1) < 64
    feature = jnp.zeros((rows, 128), f32)
    for i in range(groups // 2):
        b_even = in_ref[2 * i, :, 128:].astype(f32)
        b_odd = in_ref[2 * i + 1, :, :128].astype(f32)
        feature = feature + jnp.where(low_lane, b_odd, b_even)
        x_ref[:, 384 * i : 384 * i + 128] = in_ref[2 * i, :, :128]
        x_ref[:, 384 * i + 128 : 384 * i + 256] = jnp.where(low_lane, b_even, b_odd).astype(bf16)
        x_ref[:, 384 * i + 256 : 384 * i + 384] = in_ref[2 * i + 1, :, 128:]
    high, low = halves(jnp.sum(feature, axis=1, keepdims=True))
    lane = iota((1, 128), 1)
    x_ref[:, D:] = jnp.where(lane == 0, high, jnp.where(lane == 1, low, 0.0)).astype(bf16)


def experts(x_ref, x2_ref, gate_ref, up_ref, down_ref, keep_ref, give_ref):
    rows = x_ref.shape[0]
    feature = jnp.concatenate([x_ref[:, D:], x2_ref[:, D:]], axis=0).astype(f32)
    scale = lax.rsqrt(jnp.sum(jnp.transpose(feature), axis=0, keepdims=True) / D + epsilon)
    gate = jnp.zeros((gate_ref.shape[0], 2 * rows), f32)
    up = gate
    for n in range(DEEP):
        part = slice(n * D // DEEP, (n + 1) * D // DEEP)
        x = jnp.concatenate([x_ref[:, part], x2_ref[:, part]], axis=0)
        gate = gate + lax.dot_general(gate_ref[:, part], x, MINOR, preferred_element_type=f32)
        up = up + lax.dot_general(up_ref[:, part], x, MINOR, preferred_element_type=f32)
    gate, up = scale * gate, scale * up
    hidden = jnp.transpose(gate * jax.nn.sigmoid(gate) * up).astype(bf16)
    for n in range(WIDE):
        part = slice(n * D // WIDE, (n + 1) * D // WIDE)
        chunk = jnp.dot(hidden, down_ref[:, part], preferred_element_type=f32)
        keep_ref[:, part] = chunk[:rows]
        give_ref[:, part] = chunk[rows:].astype(bf16)


def spread(keep_ref, other_ref, out_ref):
    for i in range(D // 384):
        a, b, c = (
            keep_ref[:, 128 * n : 128 * n + 128] + other_ref[:, 128 * n : 128 * n + 128].astype(f32)
            for n in range(3 * i, 3 * i + 3)
        )
        for t in range(4):
            rows = slice(t * CAP, (t + 1) * CAP)
            out_ref[(2 * i) * 4 + t] = jnp.concatenate([a[rows], b[rows]], axis=0).astype(bf16)
            out_ref[(2 * i + 1) * 4 + t] = jnp.concatenate([b[rows], c[rows]], axis=0).astype(bf16)


def combiner(routes, weights, out_ref):
    r0, r1 = column(routes[0:1], RB).astype(jnp.int32), column(routes[1:2], RB).astype(jnp.int32)
    w0, w1 = column(weights[0:1], RB), column(weights[1:2], RB)
    place = iota((1, out_ref.shape[1]), 1)
    expert = place // 64
    chosen = jnp.where((r0 == expert) | (r1 == expert), 1.0, 0.0)
    earlier = jnp.where(iota((RB, RB), 1) < iota((RB, RB), 0), 1.0, 0.0)
    slot = jnp.dot(earlier, chosen, preferred_element_type=f32)
    weight = jnp.where(r0 == expert, w0, 0.0) + jnp.where(r1 == expert, w1, 0.0)
    row = (place % 8).astype(f32)
    for part in range(2):
        value = jnp.where(slot + part * CAP == row, weight, 0.0)
        high, rest = halves(value)
        middle, low = halves(rest)
        for n, piece in enumerate((high, middle, low)):
            out_ref[(3 * part + n) * RB : (3 * part + n + 1) * RB, :] = piece.astype(bf16)


def combine(x_ref, table_ref, own_ref, out_ref):
    odd = lax.rem(lax.axis_index("grp"), 2)
    width = out_ref.shape[1]
    x = x_ref[...].reshape(-1, 128)
    both = jnp.dot(table_ref[...], x, preferred_element_type=f32)
    a = both[2 * RB : 3 * RB] + both[RB : 2 * RB] + both[:RB]
    b = both[5 * RB :] + both[4 * RB : 5 * RB] + both[3 * RB : 4 * RB]
    mixture = jnp.concatenate([a, b], axis=1)
    mixture = jnp.where(odd == 1, pltpu.roll(mixture, width, 1), mixture)
    out_ref[...] = (own_ref[...] + mixture)[:, :width].astype(bf16)


def far(x):
    return pltpu.with_memory_space_constraint(x, pltpu.HBM)


def call(kernel, outs, specs, args, scratch=(), flops=0, moved=0, limit=8):
    single = not isinstance(outs, list)
    made = pl.pallas_call(
        kernel,
        out_shape=outs if single else tuple(outs),
        in_specs=specs,
        out_specs=VM if single else tuple(VM for _ in outs),
        scratch_shapes=list(scratch),
        compiler_params=pltpu.CompilerParams(vmem_limit_bytes=limit * 1024 * 1024),
        cost_estimate=pl.CostEstimate(flops=flops, bytes_accessed=moved, transcendentals=0),
    )
    return made(*args)


def shape(dims, dtype):
    return jax.ShapeDtypeStruct(dims, dtype)


def body(
    queries,
    new_keys,
    new_values,
    kv_memory,
    decay_rate,
    attn_gain,
    w_out,
    residual,
    moe_gain,
    w_gate,
    w_up,
    w_down,
    routes,
    route_weights,
):
    groups = lax.axis_size("grp")
    width = residual.shape[1]
    sessions, heads = queries.shape[:2]
    half = groups * sessions // 2
    turned_routes = routes.T
    swap = [(0, 1), (1, 0)]

    decay, narrow, w_turned = decay_rate.reshape(1, -1), moe_gain.reshape(1, -1), w_out.T
    held = (queries, new_keys, new_values, decay)
    passed = (w_turned, residual, narrow, turned_routes, route_weights.T)
    taken = tuple(far(x) for x in held + (attn_gain, kv_memory) + passed)
    sent, gain_near, w_near, *rest = call(
        attention,
        [shape((groups, sessions * heads, HEAD_DIM), bf16)] + [shape(x.shape, x.dtype) for x in (attn_gain,) + passed],
        [HB] * len(taken),
        taken,
        scratch=[pltpu.VMEM(x.shape, x.dtype) for x in held + (kv_memory,)]
        + [pltpu.SemaphoreType.DMA((10 + sessions,))],
        flops=10**6,
        moved=1200000,
    )
    every = lax.all_to_all(sent, "grp", 0, 0, tiled=True)
    mine, give = call(
        project,
        [shape((half, LANES), f32)] * 2,
        [VM] * 3,
        (every, w_near, gain_near),
        scratch=[pltpu.VMEM((groups * sessions * heads + 8, HEAD_DIM), f32)],
        flops=25 * 10**6,
        moved=700000,
    )
    own_rows, moe_near, table = call(
        prepare,
        [shape((RB, LANES), bf16), shape((1, LANES), f32), shape((6 * RB, 1024), bf16)],
        [VM] * 5,
        (give, *rest),
        flops=10**6,
        moved=200000,
    )
    message, summed = call(
        functools.partial(gather_side, width),
        [shape((half + RB, LANES), bf16), shape((half, LANES), f32)],
        [VM] * 3,
        (mine, lax.ppermute(give, "side", swap), own_rows),
        flops=3 * 10**10,
        moved=400000,
    )
    got = [lax.ppermute(message, "tp", [(t, (t + step) % 4) for t in range(4)]) for step in STEPS]
    outbox, own_hidden = call(
        functools.partial(dispatch, width),
        [shape((groups, 4 * CAP, LANES), bf16), shape((RB, LANES), f32)],
        [VM] * 6,
        (summed, own_rows, *got, moe_near),
        scratch=[pltpu.VMEM((half, LANES), f32)] * 2,
        flops=10**7,
        moved=700000,
    )
    inbox = lax.all_to_all(outbox, "grp", 0, 0, tiled=True)
    x_mine = call(stage, shape((4 * CAP, D + 128), bf16), [VM], (inbox,), flops=10**6, moved=500000)
    keep, give = call(
        experts,
        [shape((4 * CAP, D), f32), shape((4 * CAP, D), bf16)],
        [VM] * 5,
        (x_mine, lax.ppermute(x_mine, "side", swap), w_gate[0].T, w_up[0].T, w_down[0]),
        flops=4 * 10**8,
        moved=11000000,
        limit=12,
    )
    back = call(
        spread,
        shape((groups * 4, 2 * CAP, 128), bf16),
        [VM, VM],
        (keep, lax.ppermute(give, "side", swap)),
        flops=10**6,
        moved=900000,
    )
    returned = lax.all_to_all(back, ("grp", "tp"), 0, 0, tiled=True)
    return call(
        combine,
        shape((RB, width), bf16),
        [VM] * 3,
        (returned, table, own_hidden),
        flops=3 * 10**7,
        moved=500000,
    )


def solution(mesh):
    placed = (
        P("grp", ("side", "tp"), None),
        P("grp", ("side", "tp"), None),
        P("grp", ("side", "tp"), None),
        P("grp", ("side", "tp"), None, None),
        P(("side", "tp")),
        P(("side", "tp"), None),
        P(("side", "tp"), "grp"),
        P(("side", "tp"), "grp"),
        P("grp"),
        P("grp", None, ("side", "tp")),
        P("grp", None, ("side", "tp")),
        P("grp", ("side", "tp"), None),
        P(("side", "tp"), None),
        P(("side", "tp"), None),
    )
    return jax.shard_map(
        body, mesh=mesh, in_specs=placed, out_specs=P(("side", "tp"), "grp"), check_vma=False
    )
```

```python
import functools
import jax
import jax.numpy as jnp
from jax import lax
from jax.experimental import pallas as pl
from jax.experimental.pallas import tpu as pltpu
from jax.sharding import PartitionSpec as P

D = 6144
HEADS = 32
HEAD_DIM = 128
EXPERTS = 16
CAP = 4
RB = 16
LANES = 256
DEEP = 1
WIDE = 8

STEPS = (1, 3, 2)

epsilon = 1e-06
f32, bf16 = jnp.float32, jnp.bfloat16
VM = pl.BlockSpec(memory_space=pltpu.VMEM)
HB = pl.BlockSpec(memory_space=pltpu.HBM)
MINOR = (((1,), (1,)), ((), ()))


def iota(shape, dim):
    return lax.broadcasted_iota(jnp.int32, shape, dim)


def column(row, size):
    full = jnp.broadcast_to(row, (size, size))
    return jnp.sum(jnp.where(iota((size, size), 0) == iota((size, size), 1), full, 0.0), axis=1, keepdims=True)


def halves(value):
    high = value.astype(bf16).astype(f32)
    return high, value - high


def attention(
    q_hbm, k_hbm, v_hbm, decay_hbm, gain_hbm, kv_hbm, w_hbm, residual_hbm, moe_hbm, routes_hbm, weights_hbm,
    out_ref, gain_ref, w_ref, residual_ref, moe_ref, routes_ref, weights_ref,
    q_ref, k_ref, v_ref, decay_ref, kv_ref, sems,
):
    sessions, heads = q_ref.shape[:2]
    pairs = [(q_hbm, q_ref), (k_hbm, k_ref), (v_hbm, v_ref), (decay_hbm, decay_ref), (gain_hbm, gain_ref)]
    pairs += [(kv_hbm.at[s], kv_ref.at[s]) for s in range(sessions)]
    pairs += [(w_hbm, w_ref), (residual_hbm, residual_ref), (moe_hbm, moe_ref)]
    pairs += [(routes_hbm, routes_ref), (weights_hbm, weights_ref)]
    copies = [pltpu.make_async_copy(source, target, sems.at[i]) for i, (source, target) in enumerate(pairs)]
    for copy in copies:
        copy.start()
    for copy in copies[:5]:
        copy.wait()
    query = jnp.concatenate([q_ref[s].astype(f32) for s in range(sessions)], axis=0)
    key = jnp.concatenate([k_ref[s].astype(f32) for s in range(sessions)], axis=0)
    value = jnp.concatenate([v_ref[s].astype(f32) for s in range(sessions)], axis=0)
    dots = jnp.sum(query * key, axis=1, keepdims=True)
    count = sessions * heads
    ones = jnp.where(iota((count, count * HEAD_DIM), 1) // HEAD_DIM == iota((count, count * HEAD_DIM), 0), 1.0, 0.0)
    turned = jnp.dot(jnp.transpose(query).astype(bf16), ones.astype(bf16), preferred_element_type=f32)
    rows = []
    for s in range(sessions):
        copies[5 + s].wait()
        for h in range(heads):
            n = s * heads + h
            read = jnp.sum(turned[:, n * HEAD_DIM : (n + 1) * HEAD_DIM] * kv_ref[s, h], axis=0, keepdims=True)
            rows.append(decay_ref[:, h : h + 1] * read)
    attended = jnp.concatenate(rows, axis=0) + dots * value
    gain = jnp.concatenate([gain_ref[...]] * sessions, axis=0)
    message = (attended * gain).astype(bf16)
    for g in range(out_ref.shape[0]):
        out_ref[g] = message
    for copy in copies[5 + sessions :]:
        copy.wait()


def prepare(after_ref, residual_ref, moe_ref, routes_ref, weights_ref, own_ref, gain_ref, table_ref):
    width = residual_ref.shape[1]
    routes = routes_ref[...].astype(f32)
    lane = iota((1, LANES), 1)
    own = jnp.concatenate([residual_ref[...].astype(f32), jnp.zeros((RB, LANES - width), f32)], axis=1)
    own = jnp.where(lane == width, column(routes[0:1], RB), jnp.where(lane == width + 1, column(routes[1:2], RB), own))
    own_ref[...] = own.astype(bf16)
    gain_ref[...] = jnp.concatenate([moe_ref[...], jnp.zeros((1, LANES - width), f32)], axis=1)
    combiner(routes, weights_ref[...], table_ref)


def project(x_ref, w_ref, gain_ref, mine_ref, other_ref, spread_ref):
    heads = gain_ref.shape[0]
    width = w_ref.shape[0]
    total = x_ref.shape[0] * x_ref.shape[1]
    sessions = total // heads
    half = sessions // 2
    spread_ref[:total] = x_ref[...].reshape(total, HEAD_DIM).astype(f32)
    lane = iota((1, LANES), 1)
    squares = jnp.zeros((sessions, 1), f32)
    parts = []
    for h in range(heads):
        x = spread_ref[pl.ds(h, sessions, stride=heads), :]
        plain = x / gain_ref[h : h + 1, :]
        squares = squares + jnp.sum(plain * plain, axis=1, keepdims=True)
        parts.append(x.astype(bf16))
    projected = lax.dot_general(jnp.concatenate(parts, axis=1), w_ref[...], MINOR, preferred_element_type=f32)
    table = jnp.concatenate([projected, jnp.zeros((sessions, LANES - width), f32)], axis=1)
    table = jnp.where(lane == width, squares, table)
    first = lax.axis_index("side") == 0
    mine_ref[...] = jnp.where(first, table[:half], table[half:])
    other_ref[...] = jnp.where(first, table[half:], table[:half])


def gather_side(width, mine_ref, other_ref, own_ref, out_ref, sum_ref):
    half = mine_ref.shape[0]
    lane = iota((1, LANES), 1)
    table = mine_ref[...] + other_ref[...]
    sum_ref[...] = table
    squares = jnp.sum(jnp.where(lane == width, table, 0.0), axis=1, keepdims=True)
    high, low = halves(squares)
    table = jnp.where(lane == width, high, jnp.where(lane == width + 1, low, table)).astype(bf16)
    out_ref[:half, :] = table
    out_ref[half:, :] = own_ref[...]


def dispatch(width, sum_ref, mine_ref, a_ref, b_ref, c_ref, gain_ref, out_ref, own_ref, rest_ref, scratch_ref):
    half = sum_ref.shape[0]
    tp, odd = lax.axis_index("tp"), lax.rem(lax.axis_index("grp"), 2)
    lane = iota((1, LANES), 1)
    summed = sum_ref[...]
    rest_ref[pl.ds(pl.multiple_of(tp * RB, RB), RB), :] = mine_ref[...].astype(f32)
    for step, ref in zip(STEPS, (a_ref, b_ref, c_ref)):
        summed = summed + ref[:half, :].astype(f32)
        source = lax.rem(tp + 4 - step, 4)
        rest_ref[pl.ds(pl.multiple_of(source * RB, RB), RB), :] = ref[half:, :].astype(f32)
    squares = jnp.sum(jnp.where((lane == width) | (lane == width + 1), summed, 0.0), axis=1, keepdims=True)
    rest = rest_ref[...]
    hidden = jnp.where(lane < width, rest + lax.rsqrt(squares / (HEADS * HEAD_DIM) + epsilon) * summed, 0.0)
    scratch_ref[...] = hidden
    own_ref[...] = scratch_ref[pl.ds(pl.multiple_of(tp * RB, RB), RB), :]
    high, low = halves(jnp.sum(hidden * hidden, axis=1, keepdims=True))
    rows = jnp.where(lane == width, high, jnp.where(lane == width + 1, low, hidden * gain_ref[...]))
    rows = jnp.where(odd == 1, pltpu.roll(rows, LANES - width, 1), rows).astype(bf16)

    first = jnp.sum(jnp.where(lane == width, rest, 0.0), axis=1, keepdims=True).astype(jnp.int32)
    second = jnp.sum(jnp.where(lane == width + 1, rest, 0.0), axis=1, keepdims=True).astype(jnp.int32)
    places = EXPERTS * 4 * CAP
    place = iota((1, places), 1)
    expert = place // (4 * CAP)
    chosen = jnp.where((first == expert) | (second == expert), 1.0, 0.0)
    r, c = iota((half, half), 0), iota((half, half), 1)
    earlier = jnp.where((r // RB == c // RB) & (c < r), 1.0, 0.0).astype(bf16)
    slot = jnp.dot(earlier, chosen.astype(bf16), preferred_element_type=f32)
    block = iota((half, 1), 0) // RB
    here = (slot == (place % CAP).astype(f32)) & (block == place // CAP % 4)
    table = jnp.where(here, chosen, 0.0).astype(bf16)
    routed = lax.dot_general(table, rows, (((0,), (0,)), ((), ())), preferred_element_type=f32).astype(bf16)
    for e in range(EXPERTS):
        piece = routed[e * 4 * CAP : (e + 1) * 4 * CAP]
        out_ref[2 * e] = piece
        out_ref[2 * e + 1] = piece


def stage(in_ref, x_ref):
    groups, rows, _ = in_ref.shape
    low_lane = iota((rows, 128), 1) < 64
    feature = jnp.zeros((rows, 128), f32)
    for i in range(groups // 2):
        b_even = in_ref[2 * i, :, 128:].astype(f32)
        b_odd = in_ref[2 * i + 1, :, :128].astype(f32)
        feature = feature + jnp.where(low_lane, b_odd, b_even)
        x_ref[:, 384 * i : 384 * i + 128] = in_ref[2 * i, :, :128]
        x_ref[:, 384 * i + 128 : 384 * i + 256] = jnp.where(low_lane, b_even, b_odd).astype(bf16)
        x_ref[:, 384 * i + 256 : 384 * i + 384] = in_ref[2 * i + 1, :, 128:]
    high, low = halves(jnp.sum(feature, axis=1, keepdims=True))
    lane = iota((1, 128), 1)
    x_ref[:, D:] = jnp.where(lane == 0, high, jnp.where(lane == 1, low, 0.0)).astype(bf16)


def experts(x_ref, x2_ref, gate_ref, up_ref, down_ref, keep_ref, give_ref):
    rows = x_ref.shape[0]
    feature = jnp.concatenate([x_ref[:, D:], x2_ref[:, D:]], axis=0).astype(f32)
    scale = lax.rsqrt(jnp.sum(jnp.transpose(feature), axis=0, keepdims=True) / D + epsilon)
    gate = jnp.zeros((gate_ref.shape[0], 2 * rows), f32)
    up = gate
    for n in range(DEEP):
        part = slice(n * D // DEEP, (n + 1) * D // DEEP)
        x = jnp.concatenate([x_ref[:, part], x2_ref[:, part]], axis=0)
        gate = gate + lax.dot_general(gate_ref[:, part], x, MINOR, preferred_element_type=f32)
        up = up + lax.dot_general(up_ref[:, part], x, MINOR, preferred_element_type=f32)
    gate, up = scale * gate, scale * up
    hidden = jnp.transpose(gate * jax.nn.sigmoid(gate) * up).astype(bf16)
    for n in range(WIDE):
        part = slice(n * D // WIDE, (n + 1) * D // WIDE)
        chunk = jnp.dot(hidden, down_ref[:, part], preferred_element_type=f32)
        keep_ref[:, part] = chunk[:rows]
        give_ref[:, part] = chunk[rows:].astype(bf16)


def spread(keep_ref, other_ref, out_ref):
    for i in range(D // 384):
        a, b, c = (
            keep_ref[:, 128 * n : 128 * n + 128] + other_ref[:, 128 * n : 128 * n + 128].astype(f32)
            for n in range(3 * i, 3 * i + 3)
        )
        for t in range(4):
            rows = slice(t * CAP, (t + 1) * CAP)
            out_ref[(2 * i) * 4 + t] = jnp.concatenate([a[rows], b[rows]], axis=0).astype(bf16)
            out_ref[(2 * i + 1) * 4 + t] = jnp.concatenate([b[rows], c[rows]], axis=0).astype(bf16)


def combiner(routes, weights, out_ref):
    r0, r1 = column(routes[0:1], RB).astype(jnp.int32), column(routes[1:2], RB).astype(jnp.int32)
    w0, w1 = column(weights[0:1], RB), column(weights[1:2], RB)
    place = iota((1, out_ref.shape[1]), 1)
    expert = place // 64
    chosen = jnp.where((r0 == expert) | (r1 == expert), 1.0, 0.0)
    earlier = jnp.where(iota((RB, RB), 1) < iota((RB, RB), 0), 1.0, 0.0)
    slot = jnp.dot(earlier, chosen, preferred_element_type=f32)
    weight = jnp.where(r0 == expert, w0, 0.0) + jnp.where(r1 == expert, w1, 0.0)
    row = (place % 8).astype(f32)
    for part in range(2):
        value = jnp.where(slot + part * CAP == row, weight, 0.0)
        high, rest = halves(value)
        middle, low = halves(rest)
        for n, piece in enumerate((high, middle, low)):
            out_ref[(3 * part + n) * RB : (3 * part + n + 1) * RB, :] = piece.astype(bf16)


def combine(x_ref, table_ref, own_ref, out_ref):
    odd = lax.rem(lax.axis_index("grp"), 2)
    width = out_ref.shape[1]
    x = x_ref[...].reshape(-1, 128)
    both = jnp.dot(table_ref[...], x, preferred_element_type=f32)
    a = both[2 * RB : 3 * RB] + both[RB : 2 * RB] + both[:RB]
    b = both[5 * RB :] + both[4 * RB : 5 * RB] + both[3 * RB : 4 * RB]
    mixture = jnp.concatenate([a, b], axis=1)
    mixture = jnp.where(odd == 1, pltpu.roll(mixture, width, 1), mixture)
    out_ref[...] = (own_ref[...] + mixture)[:, :width].astype(bf16)


def far(x):
    return pltpu.with_memory_space_constraint(x, pltpu.HBM)


def call(kernel, outs, specs, args, scratch=(), flops=0, moved=0, limit=8):
    single = not isinstance(outs, list)
    made = pl.pallas_call(
        kernel,
        out_shape=outs if single else tuple(outs),
        in_specs=specs,
        out_specs=VM if single else tuple(VM for _ in outs),
        scratch_shapes=list(scratch),
        compiler_params=pltpu.CompilerParams(vmem_limit_bytes=limit * 1024 * 1024),
        cost_estimate=pl.CostEstimate(flops=flops, bytes_accessed=moved, transcendentals=0),
    )
    return made(*args)


def shape(dims, dtype):
    return jax.ShapeDtypeStruct(dims, dtype)


def body(
    queries,
    new_keys,
    new_values,
    kv_memory,
    decay_rate,
    attn_gain,
    w_out,
    residual,
    moe_gain,
    w_gate,
    w_up,
    w_down,
    routes,
    route_weights,
):
    groups = lax.axis_size("grp")
    width = residual.shape[1]
    sessions, heads = queries.shape[:2]
    half = groups * sessions // 2
    turned_routes = routes.T
    swap = [(0, 1), (1, 0)]

    decay, narrow, w_turned = decay_rate.reshape(1, -1), moe_gain.reshape(1, -1), w_out.T
    held = (queries, new_keys, new_values, decay)
    passed = (w_turned, residual, narrow, turned_routes, route_weights.T)
    taken = tuple(far(x) for x in held + (attn_gain, kv_memory) + passed)
    sent, gain_near, w_near, *rest = call(
        attention,
        [shape((groups, sessions * heads, HEAD_DIM), bf16)] + [shape(x.shape, x.dtype) for x in (attn_gain,) + passed],
        [HB] * len(taken),
        taken,
        scratch=[pltpu.VMEM(x.shape, x.dtype) for x in held + (kv_memory,)]
        + [pltpu.SemaphoreType.DMA((10 + sessions,))],
        flops=10**6,
        moved=1200000,
    )
    every = lax.all_to_all(sent, "grp", 0, 0, tiled=True)
    mine, give = call(
        project,
        [shape((half, LANES), f32)] * 2,
        [VM] * 3,
        (every, w_near, gain_near),
        scratch=[pltpu.VMEM((groups * sessions * heads + 8, HEAD_DIM), f32)],
        flops=25 * 10**6,
        moved=700000,
    )
    own_rows, moe_near, table = call(
        prepare,
        [shape((RB, LANES), bf16), shape((1, LANES), f32), shape((6 * RB, 1024), bf16)],
        [VM] * 5,
        (give, *rest),
        flops=10**6,
        moved=200000,
    )
    message, summed = call(
        functools.partial(gather_side, width),
        [shape((half + RB, LANES), bf16), shape((half, LANES), f32)],
        [VM] * 3,
        (mine, lax.ppermute(give, "side", swap), own_rows),
        flops=3 * 10**10,
        moved=400000,
    )
    got = [lax.ppermute(message, "tp", [(t, (t + step) % 4) for t in range(4)]) for step in STEPS]
    outbox, own_hidden = call(
        functools.partial(dispatch, width),
        [shape((groups, 4 * CAP, LANES), bf16), shape((RB, LANES), f32)],
        [VM] * 6,
        (summed, own_rows, *got, moe_near),
        scratch=[pltpu.VMEM((half, LANES), f32)] * 2,
        flops=10**7,
        moved=700000,
    )
    inbox = lax.all_to_all(outbox, "grp", 0, 0, tiled=True)
    x_mine = call(stage, shape((4 * CAP, D + 128), bf16), [VM], (inbox,), flops=10**6, moved=500000)
    keep, give = call(
        experts,
        [shape((4 * CAP, D), f32), shape((4 * CAP, D), bf16)],
        [VM] * 5,
        (x_mine, lax.ppermute(x_mine, "side", swap), w_gate[0].T, w_up[0].T, w_down[0]),
        flops=4 * 10**8,
        moved=11000000,
        limit=12,
    )
    back = call(
        spread,
        shape((groups * 4, 2 * CAP, 128), bf16),
        [VM, VM],
        (keep, lax.ppermute(give, "side", swap)),
        flops=10**6,
        moved=900000,
    )
    returned = lax.all_to_all(back, ("grp", "tp"), 0, 0, tiled=True)
    return call(
        combine,
        shape((RB, width), bf16),
        [VM] * 3,
        (returned, table, own_hidden),
        flops=3 * 10**7,
        moved=500000,
    )


def solution(mesh):
    placed = (
        P("grp", ("side", "tp"), None),
        P("grp", ("side", "tp"), None),
        P("grp", ("side", "tp"), None),
        P("grp", ("side", "tp"), None, None),
        P(("side", "tp")),
        P(("side", "tp"), None),
        P(("side", "tp"), "grp"),
        P(("side", "tp"), "grp"),
        P("grp"),
        P("grp", None, ("side", "tp")),
        P("grp", None, ("side", "tp")),
        P("grp", ("side", "tp"), None),
        P(("side", "tp"), None),
        P(("side", "tp"), None),
    )
    return jax.shard_map(
        body, mesh=mesh, in_specs=placed, out_specs=P(("side", "tp"), "grp"), check_vma=False
    )
```
